256 devices in a mesh: box: 64 (over z, x, core), rhs: 4 (over y).
Axes of the slice: x: 4, y: 4, z: 8, core: 2. Of those that a mesh axis runs over, the one named last changes fastest.
Arguments:
- leaf_coords: float32 [3, 131072], P(None, 'box'), may hold values from -6 to 6
- charges: float32 [32, 131072], P('rhs', 'box'), may hold values from -6 to 6
- leaf_skeleton: float32 [3, 32768], P(None, 'box'), may hold values from -6 to 6
- parent_skeleton: float32 [3, 4096], P(None, 'box'), may hold values from -6 to 6
- interp: float32 [512, 64, 256], P(('box', 'rhs')), may hold values from -0.375 to 0.375
- transfer: float32 [64, 64, 512], P('box'), may hold values from -0.25 to 0.25
- near_offset: int32 [5120, 1], replicated, may hold values from 0 to 6; in each aligned block of 80 rows (0 to 79, 80 to 159, ...) at most 16 rows name the same one
- near_partner: int32 [5120], replicated, may hold values from 0 to 7
- near_count: int32 [64], replicated, may hold values from 1 to 80, 3200 in all
- far_offset: int32 [6912, 1], replicated, may hold values from 0 to 6; in each aligned block of 108 rows (0 to 107, 108 to 215, ...) at most 21 rows name the same one
- far_partner: int32 [6912], replicated, may hold values from 0 to 8, as said below
Outputs:
- potential: float32 [32, 131072], P('rhs', 'box')
The draws below stay inside these ranges and needn't reach their ends.
Inputs may be any that keep to these rules, and one draw needn't show every extreme that they name: `near_offset`: the partner of a pair lies at owner index (own index + offset - 3) mod the number of indices of box. In each device's block of 80 rows at most 16 rows name one offset, and some offset is named by exactly that many in some block. `near_count`: live rows of each block are its first ones; some block is fully live. `far_offset`: in each device's block of 108 rows at most 21 rows name one offset, and some offset is named by exactly that many in some block. `far_partner`: rows of a leaf entry name a leaf (below 8); rows of a parent entry name a parent (from 8 on).
All inputs are finite; a program needn't handle non-finite values.
Results may differ from the reference program's by a relative error of at most 0.0001.
Values sent between devices are 32-bit elements; how exact they have to be, the bound alone decides.
A program may use at most 64 MiB of HBM per device.

```python
import math
import jax
import jax.numpy as jnp
import numpy as np
from jax import lax

LEAF = 256
SKEL = 64
LEAF_DEV = 8
NEAR_PER = 10
FAR_PER = 12
REACH = 3
PAR_DEV = 1
SK_DEV = 9
NEAR_DEV = 80
FAR_DEV = 108
CAPN = 16
CAPF = 21
LEAVES = 512
PARENTS = 64
NPTS = 131072
NRHS = 32
NEAR_ALL = 5120
FAR_ALL = 6912
N_BOX = 64


def draw_far_partner(key, part):
    key = jax.random.fold_in(key, 11)
    row_id = jnp.arange(FAR_ALL, dtype=jnp.int32) % FAR_DEV
    entry = row_id // FAR_PER
    is_leaf = entry < LEAF_DEV
    extent = jnp.where(is_leaf, LEAF_DEV, PAR_DEV).astype(jnp.int32)
    anchor = jnp.where(is_leaf, 0, LEAF_DEV).astype(jnp.int32)
    picked = jax.random.randint(key, (FAR_ALL,), 0, extent, dtype=jnp.int32)
    return (anchor + picked).astype(jnp.int32)


def touch_ends(entries, own_key, smallest, largest):
    shape = entries.shape
    spot = [jax.random.randint(jax.random.fold_in(own_key, axis), (), 0, shape[axis]) for axis in range(len(shape))]
    entries = entries.at[tuple(spot)].set(smallest)
    longest = shape.index(max(shape))
    spot[longest] = (spot[longest] + 1) % shape[longest]
    return entries.at[tuple(spot)].set(largest)


def shard_levels(key, dims, split, smallest, high):
    def one(dim, parts):
        draws = jax.random.uniform(jax.random.fold_in(jax.random.fold_in(key, 6), dim), (parts,), jnp.float32, smallest / len(split), high / len(split))
        return jnp.repeat(jnp.exp(draws), dims[dim] // parts).reshape((-1,) + (1,) * (len(dims) - dim - 1))

    factor_of = one(*split[0])
    for cut in split[1:]:
        factor_of = factor_of * one(*cut)
    return factor_of


def length_profile(number_of, total, limit, skew):
    weights = [(1 << 20) // math.isqrt(rank ** skew) + 1 for rank in range(2, number_of + 1)]
    spare, given = total - limit - (number_of - 1), [1] * (number_of - 1)
    while spare > 0:
        candidates = [i for i in range(number_of - 1) if given[i] < limit]
        whole, remaining = sum([weights[i] for i in candidates]), spare
        for i in candidates:
            extra = min(limit - given[i], max(1, remaining * weights[i] // whole), spare)
            given[i] = given[i] + extra
            spare = spare - extra
    return np.array([limit] + given)


def uneven_parts(stream_key, count, total, most, slope):
    if count == 2:
        one = jax.random.randint(stream_key, (), max(1, total - most), min(most, total - 1) + 1)
        return jnp.stack([one, total - one])
    lengths = jnp.asarray(length_profile(count, total, most, slope), jnp.int32)
    couples = (count - 1) // 2
    source_of, taker = lengths[1:1 + 2 * couples:2], lengths[2:2 + 2 * couples:2]
    room = jnp.minimum(source_of - 1, most - taker)
    shifted = jax.random.randint(jax.random.fold_in(stream_key, 1), (couples,), 0, 1 << 20) % (room + 1)
    lengths = lengths.at[1:1 + 2 * couples:2].set(source_of - shifted).at[2:2 + 2 * couples:2].set(taker + shifted)
    return lengths[jax.random.permutation(jax.random.fold_in(stream_key, 2), count)]


def assign_block(key, own, number, rows, number_of, top, bound, slope):
    order = jax.random.permutation(key, number_of)
    crowded, usual = load_shares(number_of, rows * top, bound, slope, True), load_shares(number_of, rows * top, bound, slope, False)
    places = jnp.arange(number_of)

    def named(tallies, rotation):
        used = int((tallies > 0).sum())
        fixed = max(1, used // 4)
        passed = fixed + (places - fixed + rotation * (used - fixed)) % max(1, number_of - fixed)
        return jnp.zeros((number_of,), jnp.int32).at[order[jnp.where(places < fixed, places, passed)]].set(jnp.asarray(tallies, jnp.int32))

    tallies = jnp.where(number % 4 == 0, named(crowded, number // 4), named(usual, number - number // 4 - 1))
    mixed = jax.random.permutation(jax.random.fold_in(own, 3), number_of)
    giver, taker = mixed[0:number_of // 2 * 2:2], mixed[1:number_of // 2 * 2:2]
    room = jnp.minimum(tallies[giver] - 1, bound - tallies[taker]) // 2
    room = jnp.where((giver == order[0]) | (taker == order[0]) | (tallies[taker] == 0), 0, jnp.maximum(room, 0))
    passed = jax.random.randint(jax.random.fold_in(own, 4), (number_of // 2,), 0, 1 << 20) % (room + 1)
    tallies = tallies.at[giver].add(-passed).at[taker].add(passed)
    items = jnp.searchsorted(jnp.cumsum(tallies), jnp.arange(rows * top), side="right").astype(jnp.int32)
    grid = items.reshape(top, rows).T
    grid = grid[jax.random.permutation(jax.random.fold_in(own, 1), rows)]
    rotation = jax.random.randint(jax.random.fold_in(own, 2), (rows, 1), 0, top)
    return jnp.take_along_axis(grid, (jnp.arange(top)[None, :] + rotation) % top, axis=1)


def load_shares(count, total, most, slope, full):
    weights = [(1 << 20) // math.isqrt(rank ** slope) + 1 for rank in range(1, count + 1)]
    largest = most if full else min(most, max(-(-total // count), total * weights[0] // sum(weights)))
    least = 1 if total - largest >= count - 1 else 0
    holding, spare = [largest] + [least] * (count - 1), total - largest - least * (count - 1)
    while spare > 0:
        candidates = [i for i in range(1, count) if holding[i] < largest] or [i for i in range(1, count) if holding[i] < most]
        whole, remaining = sum([weights[i] for i in candidates]), spare
        for i in candidates:
            more = min(most - holding[i], max(1, remaining * weights[i] // whole), spare)
            holding[i] = holding[i] + more
            spare = spare - more
    return np.array(holding)


def normal_values(key, shape, spread, limit, shards=(), kind=jnp.bfloat16):
    loudness = shard_levels(key, shape, shards, -0.22, 0.18) if shards else 1.0
    drawn = jax.random.normal(key, shape, jnp.float32) * spread * loudness
    return jnp.minimum(jnp.maximum(drawn, -limit), limit).astype(kind)


def setup_inputs(seed: int = 0) -> dict:
    splits = jax.random.split(jax.random.key(seed), 12)
    leaf_coords = normal_values(splits[0], (3, NPTS), 1.0, 6.0, ((1, 64),), jnp.float32)
    charges = normal_values(splits[1], (NRHS, NPTS), 1.0, 6.0, ((0, 4), (1, 64)), jnp.float32)
    leaf_skeleton = normal_values(splits[2], (3, LEAVES * SKEL), 1.0, 6.0, ((1, 64),), jnp.float32)
    parent_skeleton = normal_values(splits[3], (3, PARENTS * SKEL), 1.0, 6.0, ((1, 64),), jnp.float32)
    interp = normal_values(splits[4], (LEAVES, SKEL, LEAF), LEAF ** -0.5, 0.375, ((0, 256),), jnp.float32)
    transfer = normal_values(splits[5], (PARENTS, SKEL, 8 * SKEL), (8 * SKEL) ** -0.5, 0.25, ((0, 64),), jnp.float32)
    near_offset_keys = jax.random.split(jax.random.fold_in(splits[6], 1), NEAR_ALL // NEAR_DEV)
    near_offset_turns = jax.random.permutation(jax.random.fold_in(splits[6], 3), NEAR_ALL // NEAR_DEV)
    near_offset = jax.vmap(lambda own, number: assign_block(jax.random.fold_in(splits[6], 2), own, number, NEAR_DEV, 2 * REACH + 1, 1, CAPN, 2))(near_offset_keys, near_offset_turns).reshape((NEAR_ALL, 1))
    near_partner = touch_ends(jax.random.randint(splits[7], (NEAR_ALL,), 0, LEAF_DEV), jax.random.fold_in(splits[7], 1), 0, LEAF_DEV - 1).astype(jnp.int32)
    near_count = uneven_parts(splits[8], N_BOX, N_BOX * NEAR_DEV * 5 // 8, NEAR_DEV, 2).astype(jnp.int32)
    far_offset_keys = jax.random.split(jax.random.fold_in(splits[9], 1), FAR_ALL // FAR_DEV)
    far_offset_turns = jax.random.permutation(jax.random.fold_in(splits[9], 3), FAR_ALL // FAR_DEV)
    far_offset = jax.vmap(lambda own, number: assign_block(jax.random.fold_in(splits[9], 2), own, number, FAR_DEV, 2 * REACH + 1, 1, CAPF, 1))(far_offset_keys, far_offset_turns).reshape((FAR_ALL, 1))
    far_partner = draw_far_partner(jax.random.fold_in(splits[11], 71), 0)
    return {"leaf_coords": leaf_coords, "charges": charges, "leaf_skeleton": leaf_skeleton, "parent_skeleton": parent_skeleton, "interp": interp, "transfer": transfer, "near_offset": near_offset, "near_partner": near_partner, "near_count": near_count, "far_offset": far_offset, "far_partner": far_partner}


SOFTEN = 0.0025
COUPLE = 0.07957747154594767

def kernel_tile(sources, targets):
    differ = sources[:, :, None] - targets[:, None, :]
    square = lax.optimization_barrier(jnp.sum(differ * differ, axis=0))
    return COUPLE * lax.rsqrt(square + SOFTEN)

def pair_rows(offsets, partner, per_box, stride):
    total = offsets.shape[0]
    block_rows = total // N_BOX
    row_id = jnp.arange(total, dtype=jnp.int32)
    device = row_id // block_rows
    own_box = device * stride + row_id % block_rows // per_box
    box_owner = (device + offsets[:, 0] - REACH) % N_BOX
    return (own_box.astype(jnp.int32), (box_owner * stride + partner).astype(jnp.int32))

def pair_sweep(points, values, first, second, weight):
    highest = lax.Precision.HIGHEST

    def advance(totals, portion):
        own_index, other_index, factor = portion
        tile_set = jax.vmap(kernel_tile)(points[own_index], points[other_index])
        to_own = jnp.einsum('nab,nrb->nra', tile_set, values[other_index], precision=highest) * factor[:, None, None]
        to_other = jnp.einsum('nab,nra->nrb', tile_set, values[own_index], precision=highest) * factor[:, None, None]
        totals = totals.at[own_index].add(to_own).at[other_index].add(to_other)
        return (totals, None)
    initial = jnp.zeros_like(values)
    totals, unused = lax.scan(advance, initial, (first, second, weight))
    return totals

def reference(leaf_coords, charges, leaf_skeleton, parent_skeleton, interp, transfer, near_offset, near_partner, near_count, far_offset, far_partner):
    highest = lax.Precision.HIGHEST
    leaf_points = leaf_coords.reshape(3, LEAVES, LEAF).transpose(1, 0, 2)
    leaf_values = charges.reshape(NRHS, LEAVES, LEAF).transpose(1, 0, 2)

    def own_block(portion):
        block_points, block_values = portion
        tile_set = jax.vmap(kernel_tile)(block_points, block_points)
        return jnp.einsum('nab,nrb->nra', tile_set, block_values, precision=highest)
    self_part = lax.map(own_block, (leaf_points.reshape(N_BOX, LEAF_DEV, 3, LEAF), leaf_values.reshape(N_BOX, LEAF_DEV, NRHS, LEAF)))
    self_part = self_part.reshape(LEAVES, NRHS, LEAF)
    near_own, near_other = pair_rows(near_offset, near_partner, NEAR_PER, LEAF_DEV)
    row_id = jnp.arange(NEAR_ALL, dtype=jnp.int32)
    living = (row_id % NEAR_DEV < near_count[row_id // NEAR_DEV]).astype(leaf_coords.dtype)
    near_part = pair_sweep(leaf_points, leaf_values, near_own.reshape(N_BOX, NEAR_DEV), near_other.reshape(N_BOX, NEAR_DEV), living.reshape(N_BOX, NEAR_DEV))
    leaf_weights = jnp.einsum('lsp,lrp->lrs', interp, leaf_values, precision=highest)
    children = leaf_weights.reshape(PARENTS, 8, NRHS, SKEL).transpose(0, 2, 1, 3).reshape(PARENTS, NRHS, 8 * SKEL)
    parent_weights = jnp.einsum('ksm,krm->krs', transfer, children, precision=highest)
    leaf_table = leaf_skeleton.reshape(3, LEAVES, SKEL).transpose(1, 0, 2).reshape(N_BOX, LEAF_DEV, 3, SKEL)
    parent_table = parent_skeleton.reshape(3, PARENTS, SKEL).transpose(1, 0, 2).reshape(N_BOX, PAR_DEV, 3, SKEL)
    table_points = jnp.concatenate([leaf_table, parent_table], axis=1).reshape(N_BOX * SK_DEV, 3, SKEL)
    table_values = jnp.concatenate([leaf_weights.reshape(N_BOX, LEAF_DEV, NRHS, SKEL), parent_weights.reshape(N_BOX, PAR_DEV, NRHS, SKEL)], axis=1).reshape(N_BOX * SK_DEV, NRHS, SKEL)
    far_own, far_other = pair_rows(far_offset, far_partner, FAR_PER, SK_DEV)
    far_weight = jnp.ones((N_BOX, FAR_DEV), leaf_coords.dtype)
    coupled = pair_sweep(table_points, table_values, far_own.reshape(N_BOX, FAR_DEV), far_other.reshape(N_BOX, FAR_DEV), far_weight)
    coupled = coupled.reshape(N_BOX, SK_DEV, NRHS, SKEL)
    leaf_coupled = coupled[:, :LEAF_DEV].reshape(LEAVES, NRHS, SKEL)
    parent_coupled = coupled[:, LEAF_DEV:].reshape(PARENTS, NRHS, SKEL)
    handed = jnp.einsum('ksm,krs->krm', transfer, parent_coupled, precision=highest)
    handed = handed.reshape(PARENTS, NRHS, 8, SKEL).transpose(0, 2, 1, 3).reshape(LEAVES, NRHS, SKEL)
    leaf_down = leaf_coupled + handed
    far_part = jnp.einsum('lsp,lrs->lrp', interp, leaf_down, precision=highest)
    potential = self_part + near_part + far_part
    return potential.transpose(1, 0, 2).reshape(NRHS, NPTS)
```

```python
import functools

import jax
import jax.numpy as jnp
from jax import lax
from jax.experimental import pallas as pl
from jax.experimental.pallas import tpu as pltpu
from jax.sharding import PartitionSpec as P

REACH = 3
SPAN = 2 * REACH + 1
SOFTEN = 0.0025
COUPLE = 0.07957747154594767

LEAF = 256
SKEL = 64
LEAVES = 8
COLS = 8
NEAR_PER = 10
FAR_PER = 12
ENTRIES = 9
NEAR_ROWS = LEAVES * NEAR_PER
FAR_ROWS = ENTRIES * FAR_PER
TABLE = 640

MESH = pl.DeviceIdType.MESH
NN = (((1,), (0,)), ((), ()))
NT = (((1,), (1,)), ((), ()))
f32, bf16, i32 = jnp.float32, jnp.bfloat16, jnp.int32


def split(value):
    high = value.astype(bf16)
    low = (value - high.astype(f32)).astype(bf16)
    return high, low


def stacked(value):
    return jnp.concatenate(split(value), axis=0)


def folded(value):
    return value[:8] + value[8:16]


def mul(a, b, dims=NN):
    return lax.dot_general(a, b, dims, preferred_element_type=f32)


def lane_index(shape):
    return lax.broadcasted_iota(i32, shape, 1)


def row_index(shape):
    return lax.broadcasted_iota(i32, shape, 0)


def column_form(row, width):
    return jnp.transpose(jnp.broadcast_to(row, (128, width)))


def inverse_distance(ax, ay, az, bx, by, bz):
    dx, dy, dz = ax - bx, ay - by, az - bz
    return lax.rsqrt((dx * dx + SOFTEN) + (dy * dy + dz * dz))


def tile_pieces(spread, leaf, points, high, low):
    def piece(c):
        s = pl.ds(c * 32, 32)
        for h in range(2):
            at = slice(h * 128, h * 128 + 128)
            k = inverse_distance(
                spread[0, leaf, s, :], spread[1, leaf, s, :], spread[2, leaf, s, :],
                points[0:1, at], points[1:2, at], points[2:3, at],
            )
            high[s, at], low[s, at] = split(k)

    return [functools.partial(piece, c) for c in range(8)]


def interleave(first, second):
    each = max(1, -(-len(second) // max(1, len(first))))
    for j, step in enumerate(first):
        step()
        for other in second[j * each:(j + 1) * each]:
            other()
    for other in second[len(first) * each:]:
        other()


def kernel(
    boxes, sides,
    coords, charges, leaf_skel, parent_skel, interp, transfer,
    near_offset, near_partner, near_count, far_offset, far_partner,
    out,
    vals, pts, skel, tables, near_send, near_recv, far_send, far_recv, gathered,
    spread, spread_skel, own_v, kh0, kh1, kl0, kl1, near_x0, near_x1, own_sum,
    left_t, right_t, k_far, v_far, far_x, far_own, far_mat, ih, il, near_sum, far_sum,
    s_int, r_int, s_dat, r_dat, s_tab, r_tab, s_near, r_near, s_far, r_far,
):
    me = lax.axis_index("box")
    side = lax.axis_index("rhs")
    others = [o for o in range(SPAN) if o != REACH]

    def box_at(step):
        return lax.rem(me + (step + boxes), boxes)

    def side_at(step):
        return lax.rem(side + step, sides)

    barrier = pltpu.get_barrier_semaphore()
    for o in others:
        pl.semaphore_signal(barrier, inc=1, device_id={"box": box_at(o - REACH)}, device_id_type=MESH)
    for j in range(1, sides):
        pl.semaphore_signal(barrier, inc=1, device_id={"rhs": side_at(j)}, device_id_type=MESH)

    for leaf in range(LEAVES):
        at = slice(leaf * LEAF, (leaf + 1) * LEAF)
        own_v[leaf] = stacked(charges[:, at])
        for d in range(3):
            spread[d, leaf] = column_form(coords[d:d + 1, at], LEAF)
        vals[REACH, leaf] = charges[:, at]
        pts[REACH, leaf] = coords[:, at]
    for d in range(3):
        spread_skel[d, :LEAVES * SKEL] = column_form(leaf_skel[d:d + 1, :], LEAVES * SKEL)
        spread_skel[d, LEAVES * SKEL:] = column_form(parent_skel[d:d + 1, :], SKEL)
    skel[REACH, :, :512] = leaf_skel[...]
    skel[REACH, :, 512:] = jnp.concatenate([parent_skel[...], parent_skel[...]], axis=1)
    gathered[side] = interp[...]

    pl.semaphore_wait(barrier, len(others) + sides - 1)

    def remote(src, dst, send, recv, device):
        copy = pltpu.make_async_remote_copy(
            src_ref=src, dst_ref=dst, send_sem=send, recv_sem=recv, device_id=device, device_id_type=MESH
        )
        copy.start()
        return copy

    interp_copies = [
        remote(interp, gathered.at[side], s_int.at[j - 1], r_int.at[j - 1], {"rhs": side_at(j)})
        for j in range(1, sides)
    ]
    data_copies = []
    for o in (2, 4, 1, 5, 0, 6):
        target = {"box": box_at(REACH - o)}
        for n, src in enumerate((vals, pts, skel)):
            data_copies.append(remote(src.at[REACH], src.at[o], s_dat.at[n, o], r_dat.at[n, o], target))

    def self_pair(t, carry):
        buffers = ((kh0, kl0), (kh1, kl1))

        def matmuls(u):
            leaf = t * 2 + u
            high, low = buffers[u]

            def one():
                v = own_v[leaf]
                own_sum[leaf] = folded(mul(v, high[...], NT) + mul(v, low[...], NT))

            return [one]

        for u in range(2):
            leaf = t * 2 + u
            points = pts[REACH, leaf]
            for step in tile_pieces(spread, leaf, points, *buffers[u]):
                step()
        for u in range(2):
            matmuls(u)[0]()
        return carry

    lax.fori_loop(0, LEAVES // 2, self_pair, 0)

    left = lane_index((8, 128)) < SKEL
    for copy in interp_copies:
        copy.wait_recv()
    for m in range(4):
        high, low = split(gathered[m].reshape(128, LEAF))
        ih[m], il[m] = high, low
        both = jnp.concatenate([own_v[2 * m], own_v[2 * m + 1]], axis=0)
        got = mul(both, high, NT) + mul(both, low, NT)
        tables[REACH, :, m * 128:(m + 1) * 128] = jnp.where(left, folded(got[:16]), folded(got[16:]))
    t_high, t_low = split(transfer[0])
    children = stacked(tables[REACH, :, :LEAVES * SKEL])
    parents = folded(mul(children, t_high, NT) + mul(children, t_low, NT))
    tables[REACH, :, 512:576] = parents
    tables[REACH, :, 576:640] = jnp.zeros((COLS, SKEL), f32)
    table_copies = [
        remote(tables.at[REACH], tables.at[o], s_tab.at[o], r_tab.at[o], {"box": box_at(REACH - o)})
        for o in (2, 4, 1, 5, 0, 6)
    ]

    for copy in data_copies:
        copy.wait_recv()

    alive = near_count[me]
    near_base = me * NEAR_ROWS

    def near_leaf(leaf, carry):
        v_own = own_v[leaf]
        total = [own_sum[leaf]]
        highs, lows = (kh0, kh1), (kl0, kl1)

        def place(u):
            k = near_base + leaf * NEAR_PER + u
            return near_offset[k], near_partner[k]

        def tile(u):
            o, at = place(u)
            return tile_pieces(spread, leaf, pts[o, at], highs[u % 2], lows[u % 2])

        def matmuls(u):
            high, low = highs[u % 2], lows[u % 2]
            kept = {}

            def start():
                o, at = place(u)
                weight = jnp.where(leaf * NEAR_PER + u < alive, 1.0, 0.0).astype(f32)
                kept["v"] = stacked(vals[o, at] * weight)
                kept["other"] = mul(v_own, high[...])

            def second():
                other = folded(kept["other"] + mul(v_own, low[...]))
                at = pl.ds(pl.multiple_of((leaf * NEAR_PER + u) * 8, 8), 8)
                near_x0[at, :] = other[:, :128]
                near_x1[at, :] = other[:, 128:]

            def third():
                kept["own"] = mul(kept["v"], high[...], NT)

            def fourth():
                total[0] = total[0] + folded(kept["own"] + mul(kept["v"], low[...], NT))

            return [start, second, third, fourth]

        for step in tile(0):
            step()
        for u in range(NEAR_PER):
            interleave(matmuls(u), tile(u + 1) if u + 1 < NEAR_PER else [])
        own_sum[leaf] = total[0]
        return carry

    lax.fori_loop(0, LEAVES, near_leaf, 0)

    lanes = lane_index((1, 128))
    near_key = jnp.full((1, 128), -1, i32)
    for k in range(NEAR_ROWS):
        key = near_offset[near_base + k] * 8 + near_partner[near_base + k]
        near_key = jnp.where(lanes == k, jnp.where(k < alive, key, -1), near_key)
    chosen = jnp.where(row_index((64, 128)) == near_key, 1.0, 0.0).astype(bf16)[:, :NEAR_ROWS]
    for r in range(COLS):
        rows = pl.ds(r, NEAR_ROWS, stride=8)
        high, low = split(jnp.concatenate([near_x0[rows, :], near_x1[rows, :]], axis=1))
        reply = mul(chosen, high) + mul(chosen, low)
        for o in range(SPAN):
            for h in range(2):
                near_send[o, (2 * r + h) * 8:(2 * r + h + 1) * 8, :] = reply[8 * o:8 * o + 8, h * 128:h * 128 + 128]
    near_copies = [
        remote(near_send.at[o], near_recv.at[o], s_near.at[o], r_near.at[o], {"box": box_at(o - REACH)})
        for o in (0, 6, 1, 5, 2, 4)
    ]

    for copy in table_copies:
        copy.wait_recv()
    left3 = lane_index((3, 128)) < SKEL

    def halves(block, mask):
        turned = pltpu.roll(block, SKEL, 1)
        zero = jnp.zeros_like(block)
        even = (jnp.where(mask, block, zero), jnp.where(mask, zero, turned))
        odd = (jnp.where(mask, turned, zero), jnp.where(mask, zero, block))
        return even, odd

    def put(slot, value_pair, point_pair):
        for table, value, point in zip((left_t, right_t), value_pair, point_pair):
            table[slot, 0:8, :] = value
            table[slot, 8:11, :] = point

    for o in range(SPAN):
        for m in range(4):
            at = slice(m * 128, (m + 1) * 128)
            values = halves(tables[o, :, at], left)
            points = halves(skel[o, :, at], left3)
            for u in range(2):
                put(o * ENTRIES + 2 * m + u, values[u], points[u])
        values = halves(tables[o, :, 512:640], left)
        points = halves(skel[o, :, 512:640], left3)
        put(o * ENTRIES + LEAVES, values[0], points[0])

    far_base = me * FAR_ROWS

    def far_slot(k):
        return far_offset[far_base + k] * ENTRIES + far_partner[far_base + k]

    def far_entry(e, carry):
        mine = left_t[REACH * ENTRIES + e, 0:8, :] + right_t[REACH * ENTRIES + e, 0:8, :]
        v_own = stacked(mine)
        rows = pl.ds(pl.multiple_of(e * SKEL, SKEL), SKEL)
        for j in range(FAR_PER // 2):
            at = slice(j * 128, (j + 1) * 128)
            k = e * FAR_PER + 2 * j
            block = left_t[far_slot(k), 0:11, :] + right_t[far_slot(k + 1), 0:11, :]
            tile = inverse_distance(
                spread_skel[0, rows, :], spread_skel[1, rows, :], spread_skel[2, rows, :],
                block[8:9], block[9:10], block[10:11],
            )
            k_far[0:SKEL, at], k_far[SKEL:, at] = split(tile)
            v_far[:, at] = stacked(block[0:8])
        tiles = k_far[...]
        other = folded(mul(v_own, tiles))
        for j in range(FAR_PER // 2):
            at = pl.ds(pl.multiple_of((e * (FAR_PER // 2) + j) * 8, 8), 8)
            far_x[at, :] = other[:, j * 128:(j + 1) * 128]
        own = folded(mul(v_far[...], tiles, NT))
        far_own[e] = own + pltpu.roll(own, SKEL, 1)
        return carry

    lax.fori_loop(0, ENTRIES, far_entry, 0)

    pairs = FAR_ROWS // 2
    far_x[pairs * 8:, :] = jnp.zeros((512 - pairs * 8, 128), f32)
    keys = []
    for u in range(2):
        key_row = jnp.full((1, 128), -1, i32)
        for j in range(pairs):
            o, p = far_offset[far_base + 2 * j + u], far_partner[far_base + 2 * j + u]
            key = jnp.where(p < LEAVES, o * 8 + p, 8 * SPAN + o)
            key_row = jnp.where((lanes == j) | (lanes == j + 64), key, key_row)
        keys.append(jnp.where(row_index((64, 128)) == key_row, 1.0, 0.0).astype(bf16))
    chosen = jnp.concatenate(keys, axis=0)
    for r in range(COLS):
        high, low = split(far_x[pl.ds(r, 64, stride=8), :])
        far_mat[0:64, r * 128:(r + 1) * 128] = high
        far_mat[64:128, r * 128:(r + 1) * 128] = low
    reply = mul(chosen, far_mat[...])
    left64 = lane_index((64, 128)) < SKEL
    for m in range(4):
        a, b = slice(m * 128, (m + 1) * 128), slice((m + 4) * 128, (m + 5) * 128)
        straight = jnp.where(left64, reply[:64, a], reply[64:, b])
        crossed = jnp.where(left64, reply[:64, b], reply[64:, a])
        whole = straight + pltpu.roll(crossed, SKEL, 1)
        for o in range(SPAN):
            far_send[o, :, a] = whole[8 * o:8 * o + 8]
            far_send[o, m:m + 1, 512:640] = whole[8 * SPAN + o:8 * SPAN + o + 1]
    for o in range(SPAN):
        far_send[o, 4:8, 512:640] = jnp.zeros((4, 128), f32)
    far_copies = [
        remote(far_send.at[o], far_recv.at[o], s_far.at[o], r_far.at[o], {"box": box_at(o - REACH)})
        for o in (0, 6, 1, 5, 2, 4)
    ]

    for copy in far_copies:
        copy.wait_recv()
    total = far_send[REACH]
    for o in others:
        total = total + far_recv[o]
    for m in range(4):
        far_sum[m * 8:(m + 1) * 8, :] = total[:, m * 128:(m + 1) * 128]
    fours = total[0:4, 512:640]
    parent = jnp.concatenate([fours, pltpu.roll(fours, SKEL, 1)], axis=0) + far_own[LEAVES]
    parent = stacked(parent[:, :SKEL])
    handed = folded(mul(parent, t_high) + mul(parent, t_low))
    parts = []
    for m in range(4):
        down = handed[:, m * 128:(m + 1) * 128]
        even = far_sum[pl.ds(2 * m, 4, stride=8), :]
        odd = far_sum[pl.ds(2 * m + 1, 4, stride=8), :]
        even = jnp.concatenate([even, pltpu.roll(even, SKEL, 1)], axis=0) + far_own[2 * m] + down
        odd = jnp.concatenate([pltpu.roll(odd, SKEL, 1), odd], axis=0) + far_own[2 * m + 1] + down
        zero = jnp.zeros_like(even)
        both = jnp.concatenate([stacked(jnp.where(left, even, zero)), stacked(jnp.where(left, zero, odd))], axis=0)
        got = mul(both, ih[m]) + mul(both, il[m])
        parts += [folded(got[:16]), folded(got[16:])]

    for copy in near_copies:
        copy.wait_recv()
    total = near_send[REACH]
    for o in others:
        total = total + near_recv[o]
    near_sum[...] = total
    for leaf in range(LEAVES):
        for h in range(2):
            mine = slice(h * 128, (h + 1) * 128)
            arrived = near_sum[pl.ds(h * 8 + leaf, 8, stride=16), :]
            value = own_sum[leaf, :, mine] + arrived + parts[leaf][:, mine]
            out[:, leaf * LEAF + h * 128:leaf * LEAF + (h + 1) * 128] = COUPLE * value

    for copy in interp_copies + data_copies + table_copies + near_copies + far_copies:
        copy.wait_send()


def shards(
    leaf_coords, charges, leaf_skeleton, parent_skeleton, interp, transfer,
    near_offset, near_partner, near_count, far_offset, far_partner,
):
    boxes, sides = lax.axis_size("box"), lax.axis_size("rhs")
    vmem, smem = pl.BlockSpec(memory_space=pltpu.VMEM), pl.BlockSpec(memory_space=pltpu.SMEM)
    V, S = pltpu.VMEM, pltpu.SemaphoreType.DMA
    return pl.pallas_call(
        functools.partial(kernel, boxes, sides),
        out_shape=jax.ShapeDtypeStruct(charges.shape, f32),
        in_specs=[vmem] * 6 + [smem] * 5,
        out_specs=vmem,
        scratch_shapes=[
            V((SPAN, LEAVES, COLS, LEAF), f32),
            V((SPAN, LEAVES, 3, LEAF), f32),
            V((SPAN, 3, TABLE), f32),
            V((SPAN, COLS, TABLE), f32),
            V((SPAN, 128, 128), f32),
            V((SPAN, 128, 128), f32),
            V((SPAN, 8, TABLE), f32),
            V((SPAN, 8, TABLE), f32),
            V((4, 2, SKEL, LEAF), f32),
            V((3, LEAVES, LEAF, 128), f32),
            V((3, ENTRIES * SKEL, 128), f32),
            V((LEAVES, 16, LEAF), bf16),
            V((LEAF, LEAF), bf16),
            V((LEAF, LEAF), bf16),
            V((LEAF, LEAF), bf16),
            V((LEAF, LEAF), bf16),
            V((NEAR_ROWS * 8, 128), f32),
            V((NEAR_ROWS * 8, 128), f32),
            V((LEAVES, 8, LEAF), f32),
            V((64, 16, 128), f32),
            V((64, 16, 128), f32),
            V((128, FAR_PER * SKEL), bf16),
            V((16, FAR_PER * SKEL), bf16),
            V((512, 128), f32),
            V((ENTRIES, 8, 128), f32),
            V((128, 1024), bf16),
            V((4, 128, LEAF), bf16),
            V((4, 128, LEAF), bf16),
            V((128, 128), f32),
            V((32, 128), f32),
            S((3,)), S((3,)), S((3, SPAN)), S((3, SPAN)), S((SPAN,)), S((SPAN,)),
            S((SPAN,)), S((SPAN,)), S((SPAN,)), S((SPAN,)),
        ],
        compiler_params=pltpu.CompilerParams(
            collective_id=0, has_side_effects=True, vmem_limit_bytes=32 * 2**20
        ),
    )(
        leaf_coords, charges, leaf_skeleton, parent_skeleton, interp, transfer,
        near_offset.reshape(-1), near_partner, near_count, far_offset.reshape(-1), far_partner,
    )


def solution(mesh):
    return jax.shard_map(
        shards,
        mesh=mesh,
        in_specs=(
            P(None, "box"),
            P("rhs", "box"),
            P(None, "box"),
            P(None, "box"),
            P(("box", "rhs"), None, None),
            P("box", None, None),
            P(),
            P(),
            P(),
            P(),
            P(),
        ),
        out_specs=P("rhs", "box"),
        check_vma=False,
    )
```

```python
import functools

import jax
import jax.numpy as jnp
from jax import lax
from jax.experimental import pallas as pl
from jax.experimental.pallas import tpu as pltpu
from jax.sharding import PartitionSpec as P

REACH = 3
SPAN = 2 * REACH + 1
ORDER = (3, 2, 4, 1, 5, 0, 6)
SOFTEN = 0.0025
COUPLE = 0.07957747154594767

LEAF = 256
SKEL = 64
LEAVES = 8
COLS = 8
NEAR_PER = 10
FAR_PER = 12
ENTRIES = 9
NEAR_ROWS = LEAVES * NEAR_PER
FAR_ROWS = ENTRIES * FAR_PER
TABLE = 640

MESH = pl.DeviceIdType.MESH
NN = (((1,), (0,)), ((), ()))
NT = (((1,), (1,)), ((), ()))
f32, bf16, i32 = jnp.float32, jnp.bfloat16, jnp.int32


def split(value):
    high = value.astype(bf16)
    low = (value - high.astype(f32)).astype(bf16)
    return high, low


def stacked(value):
    return jnp.concatenate(split(value), axis=0)


def folded(value):
    return value[:8] + value[8:16]


def mul(a, b, dims=NN):
    return lax.dot_general(a, b, dims, preferred_element_type=f32)


def lane_index(shape):
    return lax.broadcasted_iota(i32, shape, 1)


def row_index(shape):
    return lax.broadcasted_iota(i32, shape, 0)


def column_form(row, width):
    return jnp.transpose(jnp.broadcast_to(row, (128, width)))


def inverse_distance(ax, ay, az, bx, by, bz):
    dx, dy, dz = ax - bx, ay - by, az - bz
    return lax.rsqrt((dx * dx + SOFTEN) + (dy * dy + dz * dz))


def tile_pieces(spread, leaf, points, high, low):
    def piece(c):
        s = pl.ds(c * 32, 32)
        for h in range(2):
            at = slice(h * 128, h * 128 + 128)
            k = inverse_distance(
                spread[0, leaf, s, :], spread[1, leaf, s, :], spread[2, leaf, s, :],
                points[0:1, at], points[1:2, at], points[2:3, at],
            )
            high[s, at], low[s, at] = split(k)

    return [functools.partial(piece, c) for c in range(8)]


def interleave(first, second):
    each = max(1, -(-len(second) // max(1, len(first))))
    for j, step in enumerate(first):
        step()
        for other in second[j * each:(j + 1) * each]:
            other()
    for other in second[len(first) * each:]:
        other()


def kernel(
    boxes, sides,
    coords, charges, leaf_skel, parent_skel, interp, transfer,
    near_offset, near_partner, near_count, far_offset, far_partner,
    out,
    val0, val1, val2, val3, val4, val5, val6,
    pts0, pts1, pts2, pts3, pts4, pts5, pts6,
    charges_v, coords_v, leaf_skel_v, parent_skel_v, transfer_v,
    noff, npart, ncount, foff, fpart, plan_v, plan,
    skel, tables, near_send, near_recv, far_send, far_recv, gathered,
    spread, spread_skel, own_v, kh0, kh1, kl0, kl1, near_run, near_own, own_sum, chosen_far,
    left_t, right_t, k_far, v_far, far_x, far_own, far_mat, ih, il, far_sum,
    s_load, s_plan, s_int, r_int, s_dat, r_dat, s_tab, r_tab, s_near, r_near, s_far, r_far,
):
    me = lax.axis_index("box")
    side = lax.axis_index("rhs")
    others = [o for o in range(SPAN) if o != REACH]
    vals = [val0, val1, val2, val3, val4, val5, val6]
    pts = [pts0, pts1, pts2, pts3, pts4, pts5, pts6]

    def box_at(step):
        return lax.rem(me + (step + boxes), boxes)

    def side_at(step):
        return lax.rem(side + step, sides)

    barrier = pltpu.get_barrier_semaphore()
    for o in others:
        pl.semaphore_signal(barrier, inc=1, device_id={"box": box_at(o - REACH)}, device_id_type=MESH)
    for j in range(1, sides):
        pl.semaphore_signal(barrier, inc=1, device_id={"rhs": side_at(j)}, device_id_type=MESH)

    loads = []
    for src, dst in (
        (charges, charges_v), (coords, coords_v), (leaf_skel, leaf_skel_v), (parent_skel, parent_skel_v),
        (near_offset, noff), (near_partner, npart), (near_count, ncount),
        (far_offset, foff), (far_partner, fpart), (interp, gathered.at[side]), (transfer, transfer_v),
    ):
        copy = pltpu.make_async_copy(src, dst, s_load.at[len(loads)])
        copy.start()
        loads.append(copy)

    for copy in loads[:4]:
        copy.wait()
    for leaf in range(LEAVES):
        at = slice(leaf * LEAF, (leaf + 1) * LEAF)
        vals[0][leaf] = charges_v[:, at]
        pts[0][leaf] = coords_v[:, at]
    skel[REACH, :, :512] = leaf_skel_v[...]
    skel[REACH, :, 512:] = jnp.concatenate([parent_skel_v[...], parent_skel_v[...]], axis=1)

    def remote(src, dst, send, recv, device):
        copy = pltpu.make_async_remote_copy(
            src_ref=src, dst_ref=dst, send_sem=send, recv_sem=recv, device_id=device, device_id_type=MESH
        )
        copy.start()
        return copy

    pl.semaphore_wait(barrier, len(others) + sides - 1)
    interp_copies = [
        remote(interp, gathered.at[side], s_int.at[j - 1], r_int.at[j - 1], {"rhs": side_at(j)})
        for j in range(1, sides)
    ]
    data_copies = [None]
    skel_copies = []
    for g in range(1, SPAN):
        target = {"box": box_at(REACH - ORDER[g])}
        data_copies.append([
            remote(src[0], src[g], s_dat.at[n, g], r_dat.at[n, g], target) for n, src in enumerate((vals, pts))
        ])
    for o in others:
        target = {"box": box_at(REACH - o)}
        skel_copies.append(remote(skel.at[REACH], skel.at[o], s_dat.at[2, o], r_dat.at[2, o], target))

    for leaf in range(LEAVES):
        at = slice(leaf * LEAF, (leaf + 1) * LEAF)
        own_v[leaf] = stacked(charges_v[:, at])
        for d in range(3):
            spread[d, leaf] = column_form(coords_v[d:d + 1, at], LEAF)

    for copy in loads[4:9]:
        copy.wait()
    alive = ncount[me]
    near_base, far_base = me * NEAR_ROWS, me * FAR_ROWS
    lanes = lane_index((1, 128))
    code = jnp.full((1, 128), 63 * 8, i32)
    for k in range(NEAR_ROWS):
        hop = noff[0, near_base + k] - REACH
        group = jnp.where(hop < 0, -2 * hop - 1, 2 * hop)
        one = group * 64 + npart[near_base + k] * 8 + k // NEAR_PER + jnp.where(k < alive, 512, 0)
        code = jnp.where(lanes == k, one, code)
    code_col = column_form(code, 128)
    pair, pair_col = (code >> 3) & 63, (code_col >> 3) & 63
    key, key_col = pair * 128 + lanes, pair_col * 128 + row_index((128, 128))
    rank = jnp.sum((key_col < key).astype(i32), axis=0, keepdims=True)
    placed = column_form(rank, 128) == lanes
    code = jnp.sum(jnp.where(placed, code_col, 0), axis=0, keepdims=True)
    before = pltpu.roll(jnp.broadcast_to(code, (8, 128)), 1, 1)[0:1]
    same = (lanes > 0) & ((code >> 3) & 63 == (before >> 3) & 63)
    upto = jnp.sum((pair_col <= lanes).astype(i32), axis=0, keepdims=True)
    named = jnp.sum((pair_col == lanes).astype(i32), axis=0, keepdims=True)
    plan_v[0:1, :] = code + jnp.where(same, 1024, 0)
    plan_v[1:2, :] = jnp.where(named > 0, upto, 0)
    plan_v[2:3, :] = rank
    plan_v[3:8, :] = jnp.zeros((5, 128), i32)
    plan_copy = pltpu.make_async_copy(plan_v, plan, s_plan)
    plan_copy.start()

    for d in range(3):
        spread_skel[d, :LEAVES * SKEL] = column_form(leaf_skel_v[d:d + 1, :], LEAVES * SKEL)
        spread_skel[d, LEAVES * SKEL:] = column_form(parent_skel_v[d:d + 1, :], SKEL)
    near_run[...] = jnp.zeros_like(near_run)
    pairs = FAR_ROWS // 2
    far_x[pairs * 8:, :] = jnp.zeros((512 - pairs * 8, 128), f32)
    for u in range(2):
        key_row = jnp.full((1, 128), -1, i32)
        for j in range(pairs):
            o, p = foff[0, far_base + 2 * j + u], fpart[far_base + 2 * j + u]
            key = jnp.where(p < LEAVES, o * 8 + p, 8 * SPAN + o)
            key_row = jnp.where((lanes == j) | (lanes == j + 64), key, key_row)
        chosen_far[u * 64:(u + 1) * 64, :] = jnp.where(row_index((64, 128)) == key_row, 1.0, 0.0).astype(bf16)

    buffers = ((kh0, kl0), (kh1, kl1))

    def self_pair(t, carry):
        for u in range(2):
            leaf = t * 2 + u
            for step in tile_pieces(spread, leaf, pts[0][leaf], *buffers[u]):
                step()
        for u in range(2):
            leaf = t * 2 + u
            high, low = buffers[u]
            v = own_v[leaf]
            own_sum[leaf] = folded(mul(v, high[...], NT) + mul(v, low[...], NT))
        return carry

    lax.fori_loop(0, LEAVES // 2, self_pair, 0)

    plan_copy.wait()
    near_copies = []

    def wait_data(g):
        for copy in data_copies[g]:
            copy.wait_recv()

    def near_phase(t, run):
        def rows_of_eight(half, run):
            first = t * 16 + half * 8
            kept_run = [run]

            def pick(bufs, code):
                group, p = (code >> 6) & 7, (code >> 3) & 7
                return jnp.where(
                    group == t, bufs[t][p], jnp.where(group == t + 1, bufs[t + 1][p], bufs[t + 2][p])
                )

            def tile(u):
                code = plan[0, first + u]
                return tile_pieces(spread, code & 7, pick(pts, code), *buffers[u % 2])

            def matmuls(u):
                high, low = buffers[u % 2]
                code = plan[0, first + u]
                kept = {}

                def start():
                    kept["own_v"] = own_v[code & 7]
                    kept["live"] = ((code >> 9) & 1).astype(f32)
                    kept["v"] = stacked(pick(vals, code) * kept["live"])
                    kept["other"] = mul(kept["own_v"], high[...])

                def second():
                    other = folded(kept["other"] + mul(kept["own_v"], low[...]))
                    again = ((code >> 10) & 1).astype(f32)
                    kept_run[0] = kept_run[0] * again + other * kept["live"]
                    near_run[first + u] = kept_run[0]

                def third():
                    kept["own"] = mul(kept["v"], high[...], NT)

                def fourth():
                    near_own[first + u] = folded(kept["own"] + mul(kept["v"], low[...], NT))

                return [start, second, third, fourth]

            for step in tile(0):
                step()
            for u in range(8):
                interleave(matmuls(u), tile(u + 1) if u + 1 < 8 else [])
            return kept_run[0]

        return lax.fori_loop(0, 2, rows_of_eight, run)

    def near_reply(g):
        for p in range(LEAVES):
            last = plan[1, g * 8 + p]
            some = jnp.where(last > 0, 1.0, 0.0).astype(f32)
            near_send[g, p] = near_run[jnp.maximum(last - 1, 0)] * some
        if g:
            near_copies.append(
                remote(near_send.at[g], near_recv.at[g], s_near.at[g], r_near.at[g], {"box": box_at(ORDER[g] - REACH)})
            )

    left = lane_index((8, 128)) < SKEL
    run = jnp.zeros((COLS, LEAF), f32)
    wait_data(1)
    wait_data(2)
    run = near_phase(0, run)
    near_reply(0)

    for copy in loads[9:]:
        copy.wait()
    for copy in interp_copies:
        copy.wait_recv()
    for m in range(4):
        high, low = split(gathered[m].reshape(128, LEAF))
        ih[m], il[m] = high, low
        both = jnp.concatenate([own_v[2 * m], own_v[2 * m + 1]], axis=0)
        got = mul(both, high, NT) + mul(both, low, NT)
        tables[REACH, :, m * 128:(m + 1) * 128] = jnp.where(left, folded(got[:16]), folded(got[16:]))
    t_high, t_low = split(transfer_v[0])
    children = stacked(tables[REACH, :, :LEAVES * SKEL])
    parents = folded(mul(children, t_high, NT) + mul(children, t_low, NT))
    tables[REACH, :, 512:576] = parents
    tables[REACH, :, 576:640] = jnp.zeros((COLS, SKEL), f32)
    table_copies = [
        remote(tables.at[REACH], tables.at[o], s_tab.at[o], r_tab.at[o], {"box": box_at(REACH - o)})
        for o in ORDER[1:]
    ]

    for t in range(1, 5):
        wait_data(t + 2)
        run = near_phase(t, run)
        near_reply(t)
    near_reply(5)
    near_reply(6)

    for copy in skel_copies + table_copies:
        copy.wait_recv()
    left3 = lane_index((3, 128)) < SKEL

    def halves(block, mask):
        turned = pltpu.roll(block, SKEL, 1)
        zero = jnp.zeros_like(block)
        even = (jnp.where(mask, block, zero), jnp.where(mask, zero, turned))
        odd = (jnp.where(mask, turned, zero), jnp.where(mask, zero, block))
        return even, odd

    def put(slot, value_pair, point_pair):
        for table, value, point in zip((left_t, right_t), value_pair, point_pair):
            table[slot, 0:8, :] = value
            table[slot, 8:11, :] = point

    for o in range(SPAN):
        for m in range(4):
            at = slice(m * 128, (m + 1) * 128)
            values = halves(tables[o, :, at], left)
            points = halves(skel[o, :, at], left3)
            for u in range(2):
                put(o * ENTRIES + 2 * m + u, values[u], points[u])
        values = halves(tables[o, :, 512:640], left)
        points = halves(skel[o, :, 512:640], left3)
        put(o * ENTRIES + LEAVES, values[0], points[0])

    def far_slot(k):
        return foff[0, far_base + k] * ENTRIES + fpart[far_base + k]

    def far_entry(e, carry):
        mine = left_t[REACH * ENTRIES + e, 0:8, :] + right_t[REACH * ENTRIES + e, 0:8, :]
        v_own = stacked(mine)
        rows = pl.ds(pl.multiple_of(e * SKEL, SKEL), SKEL)
        for j in range(FAR_PER // 2):
            at = slice(j * 128, (j + 1) * 128)
            k = e * FAR_PER + 2 * j
            block = left_t[far_slot(k), 0:11, :] + right_t[far_slot(k + 1), 0:11, :]
            tile = inverse_distance(
                spread_skel[0, rows, :], spread_skel[1, rows, :], spread_skel[2, rows, :],
                block[8:9], block[9:10], block[10:11],
            )
            k_far[0:SKEL, at], k_far[SKEL:, at] = split(tile)
            v_far[:, at] = stacked(block[0:8])
        tiles = k_far[...]
        other = folded(mul(v_own, tiles))
        for j in range(FAR_PER // 2):
            at = pl.ds(pl.multiple_of((e * (FAR_PER // 2) + j) * 8, 8), 8)
            far_x[at, :] = other[:, j * 128:(j + 1) * 128]
        own = folded(mul(v_far[...], tiles, NT))
        far_own[e] = own + pltpu.roll(own, SKEL, 1)
        return carry

    lax.fori_loop(0, ENTRIES, far_entry, 0)

    for r in range(COLS):
        high, low = split(far_x[pl.ds(r, 64, stride=8), :])
        far_mat[0:64, r * 128:(r + 1) * 128] = high
        far_mat[64:128, r * 128:(r + 1) * 128] = low
    reply = mul(chosen_far[...], far_mat[...])
    left64 = lane_index((64, 128)) < SKEL
    for m in range(4):
        a, b = slice(m * 128, (m + 1) * 128), slice((m + 4) * 128, (m + 5) * 128)
        straight = jnp.where(left64, reply[:64, a], reply[64:, b])
        crossed = jnp.where(left64, reply[:64, b], reply[64:, a])
        whole = straight + pltpu.roll(crossed, SKEL, 1)
        for o in range(SPAN):
            far_send[o, :, a] = whole[8 * o:8 * o + 8]
            far_send[o, m:m + 1, 512:640] = whole[8 * SPAN + o:8 * SPAN + o + 1]
    for o in range(SPAN):
        far_send[o, 4:8, 512:640] = jnp.zeros((4, 128), f32)
    far_copies = [
        remote(far_send.at[o], far_recv.at[o], s_far.at[o], r_far.at[o], {"box": box_at(o - REACH)})
        for o in (0, 6, 1, 5, 2, 4)
    ]

    for leaf in range(LEAVES):
        total = own_sum[leaf] + near_send[0, leaf]
        for u in range(NEAR_PER):
            total = total + near_own[plan[2, leaf * NEAR_PER + u]]
        own_sum[leaf] = total
    for copy in near_copies:
        copy.wait_recv()
    for leaf in range(LEAVES):
        total = own_sum[leaf]
        for g in range(1, SPAN):
            total = total + near_recv[g, leaf]
        own_sum[leaf] = total

    for copy in far_copies:
        copy.wait_recv()
    total = far_send[REACH]
    for o in others:
        total = total + far_recv[o]
    for m in range(4):
        far_sum[m * 8:(m + 1) * 8, :] = total[:, m * 128:(m + 1) * 128]
    fours = total[0:4, 512:640]
    parent = jnp.concatenate([fours, pltpu.roll(fours, SKEL, 1)], axis=0) + far_own[LEAVES]
    parent = stacked(parent[:, :SKEL])
    handed = folded(mul(parent, t_high) + mul(parent, t_low))
    for m in range(4):
        down = handed[:, m * 128:(m + 1) * 128]
        even = far_sum[pl.ds(2 * m, 4, stride=8), :]
        odd = far_sum[pl.ds(2 * m + 1, 4, stride=8), :]
        even = jnp.concatenate([even, pltpu.roll(even, SKEL, 1)], axis=0) + far_own[2 * m] + down
        odd = jnp.concatenate([pltpu.roll(odd, SKEL, 1), odd], axis=0) + far_own[2 * m + 1] + down
        zero = jnp.zeros_like(even)
        both = jnp.concatenate([stacked(jnp.where(left, even, zero)), stacked(jnp.where(left, zero, odd))], axis=0)
        got = mul(both, ih[m]) + mul(both, il[m])
        for u in range(2):
            leaf = 2 * m + u
            out[:, leaf * LEAF:(leaf + 1) * LEAF] = COUPLE * (own_sum[leaf] + folded(got[16 * u:16 * u + 16]))

    for copy in interp_copies + sum(data_copies[1:], []) + skel_copies + table_copies + near_copies + far_copies:
        copy.wait_send()


def shards(
    leaf_coords, charges, leaf_skeleton, parent_skeleton, interp, transfer,
    near_offset, near_partner, near_count, far_offset, far_partner,
):
    boxes, sides = lax.axis_size("box"), lax.axis_size("rhs")
    V, S, M = pltpu.VMEM, pltpu.SemaphoreType.DMA, pltpu.SMEM
    operands = (
        leaf_coords, charges, leaf_skeleton, parent_skeleton, interp, transfer,
        near_offset.reshape(1, -1), near_partner, near_count, far_offset.reshape(1, -1), far_partner,
    )
    return pl.pallas_call(
        functools.partial(kernel, boxes, sides),
        out_shape=jax.ShapeDtypeStruct(charges.shape, f32),
        in_specs=[pl.BlockSpec(memory_space=pltpu.HBM)] * len(operands),
        out_specs=pl.BlockSpec(memory_space=pltpu.VMEM),
        scratch_shapes=[V((LEAVES, COLS, LEAF), f32)] * SPAN
        + [V((LEAVES, 3, LEAF), f32)] * SPAN
        + [V(a.shape, f32) for a in (charges, leaf_coords, leaf_skeleton, parent_skeleton, transfer)]
        + [M(a.shape, i32) for a in operands[6:]]
        + [
            V((8, 128), i32),
            M((8, 128), i32),
            V((SPAN, 3, TABLE), f32),
            V((SPAN, COLS, TABLE), f32),
            V((SPAN, LEAVES, COLS, LEAF), f32),
            V((SPAN, LEAVES, COLS, LEAF), f32),
            V((SPAN, 8, TABLE), f32),
            V((SPAN, 8, TABLE), f32),
            V((4, 2, SKEL, LEAF), f32),
            V((3, LEAVES, LEAF, 128), f32),
            V((3, ENTRIES * SKEL, 128), f32),
            V((LEAVES, 16, LEAF), bf16),
            V((LEAF, LEAF), bf16),
            V((LEAF, LEAF), bf16),
            V((LEAF, LEAF), bf16),
            V((LEAF, LEAF), bf16),
            V((NEAR_ROWS, COLS, LEAF), f32),
            V((NEAR_ROWS, COLS, LEAF), f32),
            V((LEAVES, COLS, LEAF), f32),
            V((128, 128), bf16),
            V((64, 16, 128), f32),
            V((64, 16, 128), f32),
            V((128, FAR_PER * SKEL), bf16),
            V((16, FAR_PER * SKEL), bf16),
            V((512, 128), f32),
            V((ENTRIES, 8, 128), f32),
            V((128, 1024), bf16),
            V((4, 128, LEAF), bf16),
            V((4, 128, LEAF), bf16),
            V((32, 128), f32),
            S((11,)), S(()), S((3,)), S((3,)), S((3, SPAN)), S((3, SPAN)), S((SPAN,)), S((SPAN,)),
            S((SPAN,)), S((SPAN,)), S((SPAN,)), S((SPAN,)),
        ],
        compiler_params=pltpu.CompilerParams(
            collective_id=0, has_side_effects=True, vmem_limit_bytes=60 * 2**20
        ),
    )(*operands)


def solution(mesh):
    return jax.shard_map(
        shards,
        mesh=mesh,
        in_specs=(
            P(None, "box"),
            P("rhs", "box"),
            P(None, "box"),
            P(None, "box"),
            P(("box", "rhs"), None, None),
            P("box", None, None),
            P(),
            P(),
            P(),
            P(),
            P(),
        ),
        out_specs=P("rhs", "box"),
        check_vma=False,
    )
```

```python
import functools

import jax
import jax.numpy as jnp
from jax import lax
from jax.experimental import pallas as pl
from jax.experimental.pallas import tpu as pltpu
from jax.sharding import PartitionSpec as P

REACH = 3
SPAN = 2 * REACH + 1
ORDER = (4, 5, 6, 3, 2, 1, 0)
HOME = 3
AWAY = (0, 1, 2, 4, 5, 6)
SOFTEN = 0.0025
COUPLE = 0.07957747154594767

LEAF = 256
SKEL = 64
LEAVES = 8
COLS = 8
NEAR_PER = 10
FAR_PER = 12
ENTRIES = 9
NEAR_ROWS = LEAVES * NEAR_PER
FAR_ROWS = ENTRIES * FAR_PER
TABLE = 640

MESH = pl.DeviceIdType.MESH
NN = (((1,), (0,)), ((), ()))
NT = (((1,), (1,)), ((), ()))
f32, bf16, i32 = jnp.float32, jnp.bfloat16, jnp.int32


def split(value):
    high = value.astype(bf16)
    low = (value - high.astype(f32)).astype(bf16)
    return high, low


def stacked(value):
    return jnp.concatenate(split(value), axis=0)


def folded(value):
    return value[:8] + value[8:16]


def mul(a, b, dims=NN):
    return lax.dot_general(a, b, dims, preferred_element_type=f32)


def lane_index(shape):
    return lax.broadcasted_iota(i32, shape, 1)


def row_index(shape):
    return lax.broadcasted_iota(i32, shape, 0)


def column_form(row, width):
    return jnp.transpose(jnp.broadcast_to(row, (128, width)))


def inverse_distance(ax, ay, az, bx, by, bz):
    dx, dy, dz = ax - bx, ay - by, az - bz
    return lax.rsqrt((dx * dx + SOFTEN) + (dy * dy + dz * dz))


def tile_pieces(spread, leaf, points, high, low):
    def piece(c):
        s = pl.ds(c * 32, 32)
        for h in range(2):
            at = slice(h * 128, h * 128 + 128)
            k = inverse_distance(
                spread[0, leaf, s, :], spread[1, leaf, s, :], spread[2, leaf, s, :],
                points[0:1, at], points[1:2, at], points[2:3, at],
            )
            high[s, at], low[s, at] = split(k)

    return [functools.partial(piece, c) for c in range(8)]


def interleave(first, second):
    each = max(1, -(-len(second) // max(1, len(first))))
    for j, step in enumerate(first):
        step()
        for other in second[j * each:(j + 1) * each]:
            other()
    for other in second[len(first) * each:]:
        other()


def kernel(
    boxes, sides,
    coords, charges, leaf_skel, parent_skel, interp, transfer,
    near_offset, near_partner, near_count, far_offset, far_partner,
    out,
    vals_in, pts_in, vals, pts, mixed, parts, part_send, th, tl,
    charges_v, coords_v, leaf_skel_v, parent_skel_v, transfer_v,
    noff, npart, ncount, foff, fpart, plan_v, plan,
    skel, tables, near_send, near_recv, far_send, far_recv, gathered,
    spread, spread_skel, own_v, kh0, kh1, kl0, kl1, near_run, near_own, own_sum, chosen_far,
    left_t, right_t, k_far, v_far, far_x, far_own, far_mat, ih, il, far_sum,
    s_load, s_plan, s_mix, r_mix, s_part, r_part, s_int, r_int, s_dat, r_dat, s_tab, r_tab, s_near, r_near, s_far, r_far,
):
    me = lax.axis_index("box")
    side = lax.axis_index("rhs")
    others = [o for o in range(SPAN) if o != REACH]

    def box_at(step):
        return lax.rem(me + (step + boxes), boxes)

    def side_at(step):
        return lax.rem(side + step, sides)

    barrier = pltpu.get_barrier_semaphore()
    for o in others:
        pl.semaphore_signal(barrier, inc=1, device_id={"box": box_at(o - REACH)}, device_id_type=MESH)
    for j in range(1, sides):
        pl.semaphore_signal(barrier, inc=1, device_id={"rhs": side_at(j)}, device_id_type=MESH)

    loads = []
    for src, dst in (
        (charges, charges_v), (coords, coords_v), (leaf_skel, leaf_skel_v), (parent_skel, parent_skel_v),
        (near_offset, noff), (near_partner, npart), (near_count, ncount),
        (far_offset, foff), (far_partner, fpart), (interp, gathered.at[side]), (transfer, transfer_v),
    ):
        copy = pltpu.make_async_copy(src, dst, s_load.at[len(loads)])
        copy.start()
        loads.append(copy)

    for copy in loads[:4]:
        copy.wait()
    for leaf in range(LEAVES):
        at = slice(leaf * LEAF, (leaf + 1) * LEAF)
        vals_in[HOME, leaf] = charges_v[:, at]
        pts_in[HOME, leaf] = coords_v[:, at]
        vals[HOME * LEAVES + leaf] = charges_v[:, at]
        pts[HOME * LEAVES + leaf] = coords_v[:, at]
    skel[REACH, :, :512] = leaf_skel_v[...]
    skel[REACH, :, 512:] = jnp.concatenate([parent_skel_v[...], parent_skel_v[...]], axis=1)

    def remote(src, dst, send, recv, device):
        copy = pltpu.make_async_remote_copy(
            src_ref=src, dst_ref=dst, send_sem=send, recv_sem=recv, device_id=device, device_id_type=MESH
        )
        copy.start()
        return copy

    pl.semaphore_wait(barrier, len(others) + sides - 1)
    two = 2 * LEAF
    mix_copies = [
        remote(
            charges_v.at[:, pl.ds(pl.multiple_of(side_at(j) * two, two), two)], mixed.at[side],
            s_mix.at[j - 1], r_mix.at[j - 1], {"rhs": side_at(j)},
        )
        for j in range(1, sides)
    ]

    def data_copy(n, g, target):
        src = (vals_in, pts_in)[n]
        return pltpu.make_async_remote_copy(
            src_ref=src.at[HOME], dst_ref=src.at[g], send_sem=s_dat.at[n, g], recv_sem=r_dat.at[n, g],
            device_id=target, device_id_type=MESH,
        )

    data_copies, skel_copies = [], []
    for g in AWAY:
        target = {"box": box_at(REACH - ORDER[g])}
        for n in range(2):
            copy = data_copy(n, g, target)
            copy.start()
            data_copies.append(copy)
    for o in others:
        target = {"box": box_at(REACH - o)}
        skel_copies.append(remote(skel.at[REACH], skel.at[o], s_dat.at[2, o], r_dat.at[2, o], target))

    for leaf in range(LEAVES):
        at = slice(leaf * LEAF, (leaf + 1) * LEAF)
        own_v[leaf] = stacked(charges_v[:, at])
        for d in range(3):
            spread[d, leaf] = column_form(coords_v[d:d + 1, at], LEAF)

    for copy in loads[4:9]:
        copy.wait()
    alive = ncount[me]
    near_base, far_base = me * NEAR_ROWS, me * FAR_ROWS
    lanes = lane_index((1, 128))
    code = jnp.full((1, 128), 63 * 8, i32)
    for k in range(NEAR_ROWS):
        hop = noff[0, near_base + k] - REACH
        group = jnp.where(hop > 0, hop - 1, HOME - hop)
        one = group * 64 + npart[near_base + k] * 8 + k // NEAR_PER + jnp.where(k < alive, 512, 0)
        code = jnp.where(lanes == k, one, code)
    code_col = column_form(code, 128)
    pair, pair_col = (code >> 3) & 63, (code_col >> 3) & 63
    key, key_col = pair * 128 + lanes, pair_col * 128 + row_index((128, 128))
    rank = jnp.sum((key_col < key).astype(i32), axis=0, keepdims=True)
    placed = column_form(rank, 128) == lanes
    code = jnp.sum(jnp.where(placed, code_col, 0), axis=0, keepdims=True)
    before = pltpu.roll(jnp.broadcast_to(code, (8, 128)), 1, 1)[0:1]
    same = (lanes > 0) & ((code >> 3) & 63 == (before >> 3) & 63)
    upto = jnp.sum((pair_col <= lanes).astype(i32), axis=0, keepdims=True)
    named = jnp.sum((pair_col == lanes).astype(i32), axis=0, keepdims=True)
    plan_v[0:1, :] = code + jnp.where(same, 1024, 0)
    plan_v[1:2, :] = jnp.where(named > 0, upto, 0)
    plan_v[2:3, :] = rank
    plan_v[3:8, :] = jnp.zeros((5, 128), i32)
    plan_copy = pltpu.make_async_copy(plan_v, plan, s_plan)
    plan_copy.start()

    for d in range(3):
        spread_skel[d, :LEAVES * SKEL] = column_form(leaf_skel_v[d:d + 1, :], LEAVES * SKEL)
        spread_skel[d, LEAVES * SKEL:] = column_form(parent_skel_v[d:d + 1, :], SKEL)
    near_run[...] = jnp.zeros_like(near_run)
    pairs = FAR_ROWS // 2
    far_x[pairs * 8:, :] = jnp.zeros((512 - pairs * 8, 128), f32)
    for u in range(2):
        key_row = jnp.full((1, 128), -1, i32)
        for j in range(pairs):
            o, p = foff[0, far_base + 2 * j + u], fpart[far_base + 2 * j + u]
            key = jnp.where(p < LEAVES, o * 8 + p, 8 * SPAN + o)
            key_row = jnp.where((lanes == j) | (lanes == j + 64), key, key_row)
        chosen_far[u * 64:(u + 1) * 64, :] = jnp.where(row_index((64, 128)) == key_row, 1.0, 0.0).astype(bf16)

    buffers = ((kh0, kl0), (kh1, kl1))

    def self_pair(t, carry):
        for u in range(2):
            leaf = t * 2 + u
            for step in tile_pieces(spread, leaf, pts[HOME * LEAVES + leaf], *buffers[u]):
                step()
        for u in range(2):
            leaf = t * 2 + u
            high, low = buffers[u]
            v = own_v[leaf]
            own_sum[leaf] = folded(mul(v, high[...], NT) + mul(v, low[...], NT))
        return carry

    lax.fori_loop(0, LEAVES // 2, self_pair, 0)

    left = lane_index((8, 128)) < SKEL
    for copy in loads[9:]:
        copy.wait()
    mixed[side] = charges_v[:, pl.ds(pl.multiple_of(side * two, two), two)]
    for copy in mix_copies:
        copy.wait_recv()
    high, low = split(gathered[side].reshape(128, LEAF))
    columns = [
        jnp.concatenate([mixed[q, :, u * LEAF:(u + 1) * LEAF] for q in range(4)], axis=0) for u in range(2)
    ]
    both = jnp.concatenate([stacked(columns[0]), stacked(columns[1])], axis=0)
    got = mul(both, high, NT) + mul(both, low, NT)
    weights = jnp.where(
        lane_index((32, 128)) < SKEL, got[0:32] + got[32:64], got[64:96] + got[96:128]
    )
    high, low = split(transfer_v[0, :, pl.ds(pl.multiple_of(side * 128, 128), 128)])
    both = stacked(weights)
    got = mul(both, high, NT) + mul(both, low, NT)
    got = got[:32] + got[32:]
    part_send[:, 0:128] = weights
    part_send[:, 128:256] = jnp.concatenate([got, got], axis=1)
    part_copies = [
        remote(
            part_send.at[pl.ds(pl.multiple_of(side_at(j) * 8, 8), 8)], parts.at[side],
            s_part.at[j - 1], r_part.at[j - 1], {"rhs": side_at(j)},
        )
        for j in range(1, sides)
    ]
    parts[side] = part_send[pl.ds(pl.multiple_of(side * 8, 8), 8), :]
    th[...], tl[...] = split(transfer_v[0])

    plan_copy.wait()

    def arrive(g):
        here = {"box": box_at(1)}
        for n in range(2):
            data_copy(n, g, here).wait_recv()
        for leaf in range(LEAVES):
            vals[g * LEAVES + leaf] = vals_in[g, leaf]
            pts[g * LEAVES + leaf] = pts_in[g, leaf]

    def table_copy(g, step):
        slot = step + REACH
        return pltpu.make_async_remote_copy(
            src_ref=tables.at[REACH], dst_ref=tables.at[slot], send_sem=s_tab.at[slot], recv_sem=r_tab.at[slot],
            device_id={"box": box_at(-step)}, device_id_type=MESH,
        )

    def reply_copy(g, step):
        return pltpu.make_async_remote_copy(
            src_ref=near_send.at[g], dst_ref=near_recv.at[g], send_sem=s_near.at[g], recv_sem=r_near.at[g],
            device_id={"box": box_at(step)}, device_id_type=MESH,
        )

    def interp_copy(j):
        return pltpu.make_async_remote_copy(
            src_ref=interp, dst_ref=gathered.at[side], send_sem=s_int.at[j - 1], recv_sem=r_int.at[j - 1],
            device_id={"rhs": side_at(j)}, device_id_type=MESH,
        )

    def far_copy(o):
        return pltpu.make_async_remote_copy(
            src_ref=far_send.at[o], dst_ref=far_recv.at[o], send_sem=s_far.at[o], recv_sem=r_far.at[o],
            device_id={"box": box_at(o - REACH)}, device_id_type=MESH,
        )

    def near_reply(g):
        for p in range(LEAVES):
            last = plan[1, g * 8 + p]
            some = jnp.where(last > 0, 1.0, 0.0).astype(f32)
            near_send[g, p] = near_run[jnp.maximum(last - 1, 0)] * some

    def near_phase(t, run):
        @pl.when(t > 1)
        def _():
            arrive(t + 2)

        first = t * 16
        kept_run = [run]

        def tile(u):
            code = plan[0, first + u]
            return tile_pieces(spread, code & 7, pts[(code >> 3) & 63], *buffers[u % 2])

        def matmuls(u):
            high, low = buffers[u % 2]
            code = plan[0, first + u]
            kept = {}

            def start():
                kept["live"] = ((code >> 9) & 1).astype(f32)
                kept["v"] = stacked(vals[(code >> 3) & 63] * kept["live"])
                kept["own"] = mul(kept["v"], high[...], NT)

            def second():
                near_own[first + u] = folded(kept["own"] + mul(kept["v"], low[...], NT))

            def third():
                kept["own_v"] = own_v[code & 7]
                kept["other"] = mul(kept["own_v"], high[...])

            def fourth():
                other = folded(kept["other"] + mul(kept["own_v"], low[...]))
                again = ((code >> 10) & 1).astype(f32)
                kept_run[0] = kept_run[0] * again + other * kept["live"]
                near_run[first + u] = kept_run[0]

            return [start, second, third, fourth]

        for step in tile(0):
            step()
        for u in range(16):
            interleave(matmuls(u), tile(u + 1) if u + 1 < 16 else [])

        @pl.when(t < 3)
        def _():
            near_reply(t)
            reply_copy(t, t + 1).start()

        @pl.when(t == 0)
        def _():
            send_table()

        @pl.when(t == 2)
        def _():
            far_pairs()

        return kept_run[0]

    def send_table():
        for copy in part_copies:
            copy.wait_recv()
        total = parts[0, :, 128:256]
        for m in range(4):
            tables[REACH, :, m * 128:(m + 1) * 128] = parts[m, :, 0:128]
            if m:
                total = total + parts[m, :, 128:256]
        tables[REACH, :, 512:640] = total
        for g in AWAY:
            table_copy(g, ORDER[g] - REACH).start()
        for j in range(1, sides):
            interp_copy(j).start()

    def far_pairs():
        for copy in skel_copies:
            copy.wait_recv()
        for o in others:
            table_copy(0, o - REACH).wait_recv()
        left3 = lane_index((3, 128)) < SKEL

        def halves(block, mask):
            turned = pltpu.roll(block, SKEL, 1)
            zero = jnp.zeros_like(block)
            even = (jnp.where(mask, block, zero), jnp.where(mask, zero, turned))
            odd = (jnp.where(mask, turned, zero), jnp.where(mask, zero, block))
            return even, odd

        def put(slot, value_pair, point_pair):
            for table, value, point in zip((left_t, right_t), value_pair, point_pair):
                table[slot, 0:8, :] = value
                table[slot, 8:11, :] = point

        for o in range(SPAN):
            for m in range(4):
                at = slice(m * 128, (m + 1) * 128)
                values = halves(tables[o, :, at], left)
                points = halves(skel[o, :, at], left3)
                for u in range(2):
                    put(o * ENTRIES + 2 * m + u, values[u], points[u])
            values = halves(tables[o, :, 512:640], left)
            points = halves(skel[o, :, 512:640], left3)
            put(o * ENTRIES + LEAVES, values[0], points[0])

        def far_slot(k):
            return foff[0, far_base + k] * ENTRIES + fpart[far_base + k]

        def far_three(t, carry):
            def tiles(u):
                e = t * 3 + u
                rows = pl.ds(pl.multiple_of(e * SKEL, SKEL), SKEL)
                for j in range(FAR_PER // 2):
                    at = slice(j * 128, (j + 1) * 128)
                    k = e * FAR_PER + 2 * j
                    block = left_t[far_slot(k), 0:11, :] + right_t[far_slot(k + 1), 0:11, :]
                    tile = inverse_distance(
                        spread_skel[0, rows, :], spread_skel[1, rows, :], spread_skel[2, rows, :],
                        block[8:9], block[9:10], block[10:11],
                    )
                    k_far[u, 0:SKEL, at], k_far[u, SKEL:, at] = split(tile)
                    v_far[u, :, at] = stacked(block[0:8])

            def matmuls(u):
                e = t * 3 + u
                mine = left_t[REACH * ENTRIES + e, 0:8, :] + right_t[REACH * ENTRIES + e, 0:8, :]
                every = k_far[u]
                other = folded(mul(stacked(mine), every))
                for j in range(FAR_PER // 2):
                    at = pl.ds(pl.multiple_of((e * (FAR_PER // 2) + j) * 8, 8), 8)
                    far_x[at, :] = other[:, j * 128:(j + 1) * 128]
                own = folded(mul(v_far[u], every, NT))
                far_own[e] = own + pltpu.roll(own, SKEL, 1)

            tiles(0)
            tiles(1)
            matmuls(0)
            tiles(2)
            matmuls(1)
            matmuls(2)
            return carry

        lax.fori_loop(0, ENTRIES // 3, far_three, 0)

        for r in range(COLS):
            high, low = split(far_x[pl.ds(r, 64, stride=8), :])
            far_mat[0:64, r * 128:(r + 1) * 128] = high
            far_mat[64:128, r * 128:(r + 1) * 128] = low
        reply = mul(chosen_far[...], far_mat[...])
        left64 = lane_index((64, 128)) < SKEL
        for m in range(4):
            a, b = slice(m * 128, (m + 1) * 128), slice((m + 4) * 128, (m + 5) * 128)
            straight = jnp.where(left64, reply[:64, a], reply[64:, b])
            crossed = jnp.where(left64, reply[:64, b], reply[64:, a])
            whole = straight + pltpu.roll(crossed, SKEL, 1)
            for o in range(SPAN):
                far_send[o, :, a] = whole[8 * o:8 * o + 8]
                far_send[o, m:m + 1, 512:640] = whole[8 * SPAN + o:8 * SPAN + o + 1]
        for o in range(SPAN):
            far_send[o, 4:8, 512:640] = jnp.zeros((4, 128), f32)
        for o in (4, 5, 6, 2, 1, 0):
            far_copy(o).start()

    for g in range(3):
        arrive(g)
    lax.fori_loop(0, 5, near_phase, jnp.zeros((COLS, LEAF), f32))
    for g in (4, 5, 6):
        near_reply(g)
        reply_copy(g, ORDER[g] - REACH).start()
    near_reply(HOME)

    for leaf in range(LEAVES):
        total = own_sum[leaf] + near_send[HOME, leaf]
        for u in range(NEAR_PER):
            total = total + near_own[plan[2, leaf * NEAR_PER + u]]
        own_sum[leaf] = total
    for g in AWAY:
        reply_copy(g, 1).wait_recv()
    for leaf in range(LEAVES):
        total = own_sum[leaf]
        for g in AWAY:
            total = total + near_recv[g, leaf]
        own_sum[leaf] = total

    for j in range(1, sides):
        interp_copy(j).wait_recv()
    for m in range(4):
        ih[m], il[m] = split(gathered[m].reshape(128, LEAF))
    for o in others:
        far_copy(o).wait_recv()
    total = far_send[REACH]
    for o in others:
        total = total + far_recv[o]
    for m in range(4):
        far_sum[m * 8:(m + 1) * 8, :] = total[:, m * 128:(m + 1) * 128]
    fours = total[0:4, 512:640]
    parent = jnp.concatenate([fours, pltpu.roll(fours, SKEL, 1)], axis=0) + far_own[LEAVES]
    parent = stacked(parent[:, :SKEL])
    handed = folded(mul(parent, th[...]) + mul(parent, tl[...]))
    for m in range(4):
        down = handed[:, m * 128:(m + 1) * 128]
        even = far_sum[pl.ds(2 * m, 4, stride=8), :]
        odd = far_sum[pl.ds(2 * m + 1, 4, stride=8), :]
        even = jnp.concatenate([even, pltpu.roll(even, SKEL, 1)], axis=0) + far_own[2 * m] + down
        odd = jnp.concatenate([pltpu.roll(odd, SKEL, 1), odd], axis=0) + far_own[2 * m + 1] + down
        zero = jnp.zeros_like(even)
        both = jnp.concatenate([stacked(jnp.where(left, even, zero)), stacked(jnp.where(left, zero, odd))], axis=0)
        got = mul(both, ih[m]) + mul(both, il[m])
        for u in range(2):
            leaf = 2 * m + u
            out[:, leaf * LEAF:(leaf + 1) * LEAF] = COUPLE * (own_sum[leaf] + folded(got[16 * u:16 * u + 16]))

    for copy in mix_copies + data_copies + skel_copies + part_copies:
        copy.wait_send()
    for j in range(1, sides):
        interp_copy(j).wait_send()
    for g in AWAY:
        step = ORDER[g] - REACH
        table_copy(g, step).wait_send()
        reply_copy(g, step).wait_send()
        far_copy(ORDER[g]).wait_send()


def shards(
    leaf_coords, charges, leaf_skeleton, parent_skeleton, interp, transfer,
    near_offset, near_partner, near_count, far_offset, far_partner,
):
    boxes, sides = lax.axis_size("box"), lax.axis_size("rhs")
    V, S, M = pltpu.VMEM, pltpu.SemaphoreType.DMA, pltpu.SMEM
    operands = (
        leaf_coords, charges, leaf_skeleton, parent_skeleton, interp, transfer,
        near_offset.reshape(1, -1), near_partner, near_count, far_offset.reshape(1, -1), far_partner,
    )
    return pl.pallas_call(
        functools.partial(kernel, boxes, sides),
        out_shape=jax.ShapeDtypeStruct(charges.shape, f32),
        in_specs=[pl.BlockSpec(memory_space=pltpu.HBM)] * len(operands),
        out_specs=pl.BlockSpec(memory_space=pltpu.VMEM),
        scratch_shapes=[
            V((SPAN, LEAVES, COLS, LEAF), f32),
            V((SPAN, LEAVES, 3, LEAF), f32),
            V((SPAN * LEAVES, COLS, LEAF), f32),
            V((SPAN * LEAVES, 3, LEAF), f32),
            V((4, COLS, 2 * LEAF), f32),
            V((4, COLS, 256), f32),
            V((32, 256), f32),
            V((SKEL, 512), bf16),
            V((SKEL, 512), bf16),
        ]
        + [V(a.shape, f32) for a in (charges, leaf_coords, leaf_skeleton, parent_skeleton, transfer)]
        + [M(a.shape, i32) for a in operands[6:]]
        + [
            V((8, 128), i32),
            M((8, 128), i32),
            V((SPAN, 3, TABLE), f32),
            V((SPAN, COLS, TABLE), f32),
            V((SPAN, LEAVES, COLS, LEAF), f32),
            V((SPAN, LEAVES, COLS, LEAF), f32),
            V((SPAN, 8, TABLE), f32),
            V((SPAN, 8, TABLE), f32),
            V((4, 2, SKEL, LEAF), f32),
            V((3, LEAVES, LEAF, 128), f32),
            V((3, ENTRIES * SKEL, 128), f32),
            V((LEAVES, 16, LEAF), bf16),
            V((LEAF, LEAF), bf16),
            V((LEAF, LEAF), bf16),
            V((LEAF, LEAF), bf16),
            V((LEAF, LEAF), bf16),
            V((NEAR_ROWS, COLS, LEAF), f32),
            V((NEAR_ROWS, COLS, LEAF), f32),
            V((LEAVES, COLS, LEAF), f32),
            V((128, 128), bf16),
            V((64, 16, 128), f32),
            V((64, 16, 128), f32),
            V((3, 128, FAR_PER * SKEL), bf16),
            V((3, 16, FAR_PER * SKEL), bf16),
            V((512, 128), f32),
            V((ENTRIES, 8, 128), f32),
            V((128, 1024), bf16),
            V((4, 128, LEAF), bf16),
            V((4, 128, LEAF), bf16),
            V((32, 128), f32),
            S((11,)), S(()), S((3,)), S((3,)), S((3,)), S((3,)), S((3,)), S((3,)), S((3, SPAN)), S((3, SPAN)), S((SPAN,)), S((SPAN,)),
            S((SPAN,)), S((SPAN,)), S((SPAN,)), S((SPAN,)),
        ],
        compiler_params=pltpu.CompilerParams(
            collective_id=0, has_side_effects=True, vmem_limit_bytes=60 * 2**20
        ),
    )(*operands)


def solution(mesh):
    return jax.shard_map(
        shards,
        mesh=mesh,
        in_specs=(
            P(None, "box"),
            P("rhs", "box"),
            P(None, "box"),
            P(None, "box"),
            P(("box", "rhs"), None, None),
            P("box", None, None),
            P(),
            P(),
            P(),
            P(),
            P(),
        ),
        out_specs=P("rhs", "box"),
        check_vma=False,
    )
```

```python
import functools

import jax
import jax.numpy as jnp
from jax import lax
from jax.experimental import pallas as pl
from jax.experimental.pallas import tpu as pltpu
from jax.sharding import PartitionSpec as P

REACH = 3
SPAN = 2 * REACH + 1
ORDER = (4, 5, 6, 3, 2, 1, 0)
HOME = 3
AWAY = (0, 1, 2, 4, 5, 6)
SOFTEN = 0.0025
COUPLE = 0.07957747154594767

LEAF = 256
SKEL = 64
LEAVES = 8
COLS = 8
NEAR_PER = 10
FAR_PER = 12
ENTRIES = 9
NEAR_ROWS = LEAVES * NEAR_PER
FAR_ROWS = ENTRIES * FAR_PER
TABLE = 640

MESH = pl.DeviceIdType.MESH
NN = (((1,), (0,)), ((), ()))
NT = (((1,), (1,)), ((), ()))
f32, bf16, i32 = jnp.float32, jnp.bfloat16, jnp.int32


def split(value):
    high = value.astype(bf16)
    low = (value - high.astype(f32)).astype(bf16)
    return high, low


def stacked(value):
    return jnp.concatenate(split(value), axis=0)


def folded(value):
    return value[:8] + value[8:16]


def mul(a, b, dims=NN):
    return lax.dot_general(a, b, dims, preferred_element_type=f32)


def lane_index(shape):
    return lax.broadcasted_iota(i32, shape, 1)


def row_index(shape):
    return lax.broadcasted_iota(i32, shape, 0)


def column_form(row, width):
    return jnp.transpose(jnp.broadcast_to(row, (128, width)))


def inverse_distance(ax, ay, az, bx, by, bz):
    dx, dy, dz = ax - bx, ay - by, az - bz
    return lax.rsqrt((dx * dx + SOFTEN) + (dy * dy + dz * dz))


def tile_pieces(spread, leaf, points, high, low):
    def piece(c):
        s = pl.ds(c * 32, 32)
        for h in range(2):
            at = slice(h * 128, h * 128 + 128)
            k = inverse_distance(
                spread[0, leaf, s, :], spread[1, leaf, s, :], spread[2, leaf, s, :],
                points[0:1, at], points[1:2, at], points[2:3, at],
            )
            high[s, at], low[s, at] = split(k)

    return [functools.partial(piece, c) for c in range(8)]


def interleave(first, second):
    each = max(1, -(-len(second) // max(1, len(first))))
    for j, step in enumerate(first):
        step()
        for other in second[j * each:(j + 1) * each]:
            other()
    for other in second[len(first) * each:]:
        other()


def kernel(
    boxes, sides,
    coords, charges, leaf_skel, parent_skel, interp, transfer,
    near_offset, near_partner, near_count, far_offset, far_partner,
    out,
    vals_in, pts_in, vals, pts, mixed, parts, part_send, th, tl,
    charges_v, coords_v, leaf_skel_v, parent_skel_v, transfer_v,
    noff, npart, ncount, foff, fpart, plan_v, plan,
    skel, tables, near_send, near_recv, far_send, far_recv, gathered,
    spread, spread_skel, own_v, kh0, kh1, kl0, kl1, near_run, near_own, own_sum, chosen_far,
    left_t, right_t, k_far, v_far, far_x, far_own, far_mat, ih, il, far_sum,
    s_load, s_plan, s_mix, r_mix, s_part, r_part, s_int, r_int, s_dat, r_dat, s_tab, r_tab, s_near, r_near, s_far, r_far,
):
    me = lax.axis_index("box")
    side = lax.axis_index("rhs")
    others = [o for o in range(SPAN) if o != REACH]

    def box_at(step):
        return lax.rem(me + (step + boxes), boxes)

    def side_at(step):
        return lax.rem(side + step, sides)

    barrier = pltpu.get_barrier_semaphore()
    for o in others:
        pl.semaphore_signal(barrier, inc=1, device_id={"box": box_at(o - REACH)}, device_id_type=MESH)
    for j in range(1, sides):
        pl.semaphore_signal(barrier, inc=1, device_id={"rhs": side_at(j)}, device_id_type=MESH)

    loads = []
    for src, dst in (
        (charges, charges_v), (coords, coords_v), (leaf_skel, leaf_skel_v), (parent_skel, parent_skel_v),
        (near_offset, noff), (near_partner, npart), (near_count, ncount),
        (far_offset, foff), (far_partner, fpart), (interp, gathered.at[side]), (transfer, transfer_v),
    ):
        copy = pltpu.make_async_copy(src, dst, s_load.at[len(loads)])
        copy.start()
        loads.append(copy)

    for copy in loads[:4]:
        copy.wait()
    for leaf in range(LEAVES):
        at = slice(leaf * LEAF, (leaf + 1) * LEAF)
        vals_in[HOME, leaf] = charges_v[:, at]
        pts_in[HOME, leaf] = coords_v[:, at]
        vals[HOME * LEAVES + leaf] = charges_v[:, at]
        pts[HOME * LEAVES + leaf] = coords_v[:, at]
    skel[REACH, :, :512] = leaf_skel_v[...]
    skel[REACH, :, 512:] = jnp.concatenate([parent_skel_v[...], parent_skel_v[...]], axis=1)

    def remote(src, dst, send, recv, device):
        copy = pltpu.make_async_remote_copy(
            src_ref=src, dst_ref=dst, send_sem=send, recv_sem=recv, device_id=device, device_id_type=MESH
        )
        copy.start()
        return copy

    pl.semaphore_wait(barrier, len(others) + sides - 1)
    two = 2 * LEAF
    mix_copies = [
        remote(
            charges_v.at[:, pl.ds(pl.multiple_of(side_at(j) * two, two), two)], mixed.at[side],
            s_mix.at[j - 1], r_mix.at[j - 1], {"rhs": side_at(j)},
        )
        for j in range(1, sides)
    ]

    def data_copy(n, g, target):
        src = (vals_in, pts_in)[n]
        return pltpu.make_async_remote_copy(
            src_ref=src.at[HOME], dst_ref=src.at[g], send_sem=s_dat.at[n, g], recv_sem=r_dat.at[n, g],
            device_id=target, device_id_type=MESH,
        )

    data_copies, skel_copies = [], []
    for g in AWAY:
        target = {"box": box_at(REACH - ORDER[g])}
        for n in range(2):
            copy = data_copy(n, g, target)
            copy.start()
            data_copies.append(copy)
    for o in others:
        target = {"box": box_at(REACH - o)}
        skel_copies.append(remote(skel.at[REACH], skel.at[o], s_dat.at[2, o], r_dat.at[2, o], target))

    for leaf in range(LEAVES):
        at = slice(leaf * LEAF, (leaf + 1) * LEAF)
        own_v[leaf] = stacked(charges_v[:, at])
        for d in range(3):
            spread[d, leaf] = column_form(coords_v[d:d + 1, at], LEAF)

    for copy in loads[4:9]:
        copy.wait()
    alive = ncount[me]
    near_base, far_base = me * NEAR_ROWS, me * FAR_ROWS
    lanes = lane_index((1, 128))
    code = jnp.full((1, 128), 63 * 8, i32)
    for k in range(NEAR_ROWS):
        hop = noff[0, near_base + k] - REACH
        group = jnp.where(hop > 0, hop - 1, HOME - hop)
        one = group * 64 + npart[near_base + k] * 8 + k // NEAR_PER + jnp.where(k < alive, 512, 0)
        code = jnp.where(lanes == k, one, code)
    code_col = column_form(code, 128)
    pair, pair_col = (code >> 3) & 63, (code_col >> 3) & 63
    key, key_col = pair * 128 + lanes, pair_col * 128 + row_index((128, 128))
    rank = jnp.sum((key_col < key).astype(i32), axis=0, keepdims=True)
    placed = column_form(rank, 128) == lanes
    code = jnp.sum(jnp.where(placed, code_col, 0), axis=0, keepdims=True)
    before = pltpu.roll(jnp.broadcast_to(code, (8, 128)), 1, 1)[0:1]
    same = (lanes > 0) & ((code >> 3) & 63 == (before >> 3) & 63)
    upto = jnp.sum((pair_col <= lanes).astype(i32), axis=0, keepdims=True)
    named = jnp.sum((pair_col == lanes).astype(i32), axis=0, keepdims=True)
    plan_v[0:1, :] = code + jnp.where(same, 1024, 0)
    plan_v[1:2, :] = jnp.where(named > 0, upto, 0)
    plan_v[2:3, :] = rank
    plan_v[3:8, :] = jnp.zeros((5, 128), i32)
    plan_copy = pltpu.make_async_copy(plan_v, plan, s_plan)
    plan_copy.start()

    left = lane_index((8, 128)) < SKEL
    for copy in loads[9:]:
        copy.wait()
    mixed[side] = charges_v[:, pl.ds(pl.multiple_of(side * two, two), two)]
    for copy in mix_copies:
        copy.wait_recv()
    high, low = split(gathered[side].reshape(128, LEAF))
    columns = [
        jnp.concatenate([mixed[q, :, u * LEAF:(u + 1) * LEAF] for q in range(4)], axis=0) for u in range(2)
    ]
    both = jnp.concatenate([stacked(columns[0]), stacked(columns[1])], axis=0)
    got = mul(both, high, NT) + mul(both, low, NT)
    weights = jnp.where(
        lane_index((32, 128)) < SKEL, got[0:32] + got[32:64], got[64:96] + got[96:128]
    )
    high, low = split(transfer_v[0, :, pl.ds(pl.multiple_of(side * 128, 128), 128)])
    both = stacked(weights)
    got = mul(both, high, NT) + mul(both, low, NT)
    got = got[:32] + got[32:]
    part_send[:, 0:128] = weights
    part_send[:, 128:256] = jnp.concatenate([got, got], axis=1)
    part_copies = [
        remote(
            part_send.at[pl.ds(pl.multiple_of(side_at(j) * 8, 8), 8)], parts.at[side],
            s_part.at[j - 1], r_part.at[j - 1], {"rhs": side_at(j)},
        )
        for j in range(1, sides)
    ]
    parts[side] = part_send[pl.ds(pl.multiple_of(side * 8, 8), 8), :]
    th[...], tl[...] = split(transfer_v[0])

    buffers = ((kh0, kl0), (kh1, kl1))

    def self_pair(t, carry):
        for u in range(2):
            leaf = t * 2 + u
            for step in tile_pieces(spread, leaf, pts[HOME * LEAVES + leaf], *buffers[u]):
                step()
        for u in range(2):
            leaf = t * 2 + u
            high, low = buffers[u]
            v = own_v[leaf]
            own_sum[leaf] = folded(mul(v, high[...], NT) + mul(v, low[...], NT))
        return carry

    lax.fori_loop(0, LEAVES // 2, self_pair, 0)

    for d in range(3):
        spread_skel[d, :LEAVES * SKEL] = column_form(leaf_skel_v[d:d + 1, :], LEAVES * SKEL)
        spread_skel[d, LEAVES * SKEL:] = column_form(parent_skel_v[d:d + 1, :], SKEL)
    near_run[...] = jnp.zeros_like(near_run)
    pairs = FAR_ROWS // 2
    far_x[pairs * 8:, :] = jnp.zeros((512 - pairs * 8, 128), f32)
    for u in range(2):
        key_row = jnp.full((1, 128), -1, i32)
        for j in range(pairs):
            o, p = foff[0, far_base + 2 * j + u], fpart[far_base + 2 * j + u]
            key = jnp.where(p < LEAVES, o * 8 + p, 8 * SPAN + o)
            key_row = jnp.where((lanes == j) | (lanes == j + 64), key, key_row)
        chosen_far[u * 64:(u + 1) * 64, :] = jnp.where(row_index((64, 128)) == key_row, 1.0, 0.0).astype(bf16)

    plan_copy.wait()

    def arrive(g):
        here = {"box": box_at(1)}
        for n in range(2):
            data_copy(n, g, here).wait_recv()
        for leaf in range(LEAVES):
            vals[g * LEAVES + leaf] = vals_in[g, leaf]
            pts[g * LEAVES + leaf] = pts_in[g, leaf]

    def table_copy(g, step):
        slot = step + REACH
        return pltpu.make_async_remote_copy(
            src_ref=tables.at[REACH], dst_ref=tables.at[slot], send_sem=s_tab.at[slot], recv_sem=r_tab.at[slot],
            device_id={"box": box_at(-step)}, device_id_type=MESH,
        )

    def reply_copy(g, step):
        return pltpu.make_async_remote_copy(
            src_ref=near_send.at[g], dst_ref=near_recv.at[g], send_sem=s_near.at[g], recv_sem=r_near.at[g],
            device_id={"box": box_at(step)}, device_id_type=MESH,
        )

    def interp_copy(j):
        return pltpu.make_async_remote_copy(
            src_ref=interp, dst_ref=gathered.at[side], send_sem=s_int.at[j - 1], recv_sem=r_int.at[j - 1],
            device_id={"rhs": side_at(j)}, device_id_type=MESH,
        )

    def far_copy(o):
        return pltpu.make_async_remote_copy(
            src_ref=far_send.at[o], dst_ref=far_recv.at[o], send_sem=s_far.at[o], recv_sem=r_far.at[o],
            device_id={"box": box_at(o - REACH)}, device_id_type=MESH,
        )

    def near_reply(g):
        for p in range(LEAVES):
            last = plan[1, g * 8 + p]
            some = jnp.where(last > 0, 1.0, 0.0).astype(f32)
            near_send[g, p] = near_run[jnp.maximum(last - 1, 0)] * some

    def near_phase(t, run):
        @pl.when(t > 1)
        def _():
            arrive(t + 2)

        first = t * 16
        kept_run = [run]

        def tile(u):
            code = plan[0, first + u]
            return tile_pieces(spread, code & 7, pts[(code >> 3) & 63], *buffers[u % 2])

        def matmuls(u):
            high, low = buffers[u % 2]
            code = plan[0, first + u]
            kept = {}

            def start():
                kept["live"] = ((code >> 9) & 1).astype(f32)
                kept["v"] = stacked(vals[(code >> 3) & 63] * kept["live"])
                kept["own"] = mul(kept["v"], high[...], NT)

            def second():
                near_own[first + u] = folded(kept["own"] + mul(kept["v"], low[...], NT))

            def third():
                kept["own_v"] = own_v[code & 7]
                kept["other"] = mul(kept["own_v"], high[...])

            def fourth():
                other = folded(kept["other"] + mul(kept["own_v"], low[...]))
                again = ((code >> 10) & 1).astype(f32)
                kept_run[0] = kept_run[0] * again + other * kept["live"]
                near_run[first + u] = kept_run[0]

            return [start, second, third, fourth]

        for step in tile(0):
            step()
        for u in range(16):
            interleave(matmuls(u), tile(u + 1) if u + 1 < 16 else [])

        @pl.when(t < 3)
        def _():
            near_reply(t)
            reply_copy(t, t + 1).start()

        @pl.when(t == 1)
        def _():
            far_pairs()

        return kept_run[0]

    def send_table():
        for copy in part_copies:
            copy.wait_recv()
        total = parts[0, :, 128:256]
        for m in range(4):
            tables[REACH, :, m * 128:(m + 1) * 128] = parts[m, :, 0:128]
            if m:
                total = total + parts[m, :, 128:256]
        tables[REACH, :, 512:640] = total
        for g in AWAY:
            table_copy(g, ORDER[g] - REACH).start()
        for j in range(1, sides):
            interp_copy(j).start()

    def far_pairs():
        for copy in skel_copies:
            copy.wait_recv()
        for o in others:
            table_copy(0, o - REACH).wait_recv()
        left3 = lane_index((3, 128)) < SKEL

        def halves(block, mask):
            turned = pltpu.roll(block, SKEL, 1)
            zero = jnp.zeros_like(block)
            even = (jnp.where(mask, block, zero), jnp.where(mask, zero, turned))
            odd = (jnp.where(mask, turned, zero), jnp.where(mask, zero, block))
            return even, odd

        def put(slot, value_pair, point_pair):
            for table, value, point in zip((left_t, right_t), value_pair, point_pair):
                table[slot, 0:8, :] = value
                table[slot, 8:11, :] = point

        for o in range(SPAN):
            for m in range(4):
                at = slice(m * 128, (m + 1) * 128)
                values = halves(tables[o, :, at], left)
                points = halves(skel[o, :, at], left3)
                for u in range(2):
                    put(o * ENTRIES + 2 * m + u, values[u], points[u])
            values = halves(tables[o, :, 512:640], left)
            points = halves(skel[o, :, 512:640], left3)
            put(o * ENTRIES + LEAVES, values[0], points[0])

        def far_slot(k):
            return foff[0, far_base + k] * ENTRIES + fpart[far_base + k]

        def far_three(t, carry):
            def tiles(u):
                e = t * 3 + u
                rows = pl.ds(pl.multiple_of(e * SKEL, SKEL), SKEL)
                for j in range(FAR_PER // 2):
                    at = slice(j * 128, (j + 1) * 128)
                    k = e * FAR_PER + 2 * j
                    block = left_t[far_slot(k), 0:11, :] + right_t[far_slot(k + 1), 0:11, :]
                    tile = inverse_distance(
                        spread_skel[0, rows, :], spread_skel[1, rows, :], spread_skel[2, rows, :],
                        block[8:9], block[9:10], block[10:11],
                    )
                    k_far[u, 0:SKEL, at], k_far[u, SKEL:, at] = split(tile)
                    v_far[u, :, at] = stacked(block[0:8])

            def matmuls(u):
                e = t * 3 + u
                mine = left_t[REACH * ENTRIES + e, 0:8, :] + right_t[REACH * ENTRIES + e, 0:8, :]
                every = k_far[u]
                other = folded(mul(stacked(mine), every))
                for j in range(FAR_PER // 2):
                    at = pl.ds(pl.multiple_of((e * (FAR_PER // 2) + j) * 8, 8), 8)
                    far_x[at, :] = other[:, j * 128:(j + 1) * 128]
                own = folded(mul(v_far[u], every, NT))
                far_own[e] = own + pltpu.roll(own, SKEL, 1)

            tiles(0)
            tiles(1)
            matmuls(0)
            tiles(2)
            matmuls(1)
            matmuls(2)
            return carry

        lax.fori_loop(0, ENTRIES // 3, far_three, 0)

        for r in range(COLS):
            high, low = split(far_x[pl.ds(r, 64, stride=8), :])
            far_mat[0:64, r * 128:(r + 1) * 128] = high
            far_mat[64:128, r * 128:(r + 1) * 128] = low
        reply = mul(chosen_far[...], far_mat[...])
        left64 = lane_index((64, 128)) < SKEL
        for m in range(4):
            a, b = slice(m * 128, (m + 1) * 128), slice((m + 4) * 128, (m + 5) * 128)
            straight = jnp.where(left64, reply[:64, a], reply[64:, b])
            crossed = jnp.where(left64, reply[:64, b], reply[64:, a])
            whole = straight + pltpu.roll(crossed, SKEL, 1)
            for o in range(SPAN):
                far_send[o, :, a] = whole[8 * o:8 * o + 8]
                far_send[o, m:m + 1, 512:640] = whole[8 * SPAN + o:8 * SPAN + o + 1]
        for o in range(SPAN):
            far_send[o, 4:8, 512:640] = jnp.zeros((4, 128), f32)
        for o in (4, 5, 6, 2, 1, 0):
            far_copy(o).start()

    send_table()
    for g in range(3):
        arrive(g)
    lax.fori_loop(0, 5, near_phase, jnp.zeros((COLS, LEAF), f32))
    for g in (4, 5, 6):
        near_reply(g)
        reply_copy(g, ORDER[g] - REACH).start()
    near_reply(HOME)

    for leaf in range(LEAVES):
        total = own_sum[leaf] + near_send[HOME, leaf]
        for u in range(NEAR_PER):
            total = total + near_own[plan[2, leaf * NEAR_PER + u]]
        own_sum[leaf] = total
    for j in range(1, sides):
        interp_copy(j).wait_recv()
    for m in range(4):
        ih[m], il[m] = split(gathered[m].reshape(128, LEAF))
    for o in others:
        far_copy(o).wait_recv()
    total = far_send[REACH]
    for o in others:
        total = total + far_recv[o]
    for m in range(4):
        far_sum[m * 8:(m + 1) * 8, :] = total[:, m * 128:(m + 1) * 128]
    fours = total[0:4, 512:640]
    parent = jnp.concatenate([fours, pltpu.roll(fours, SKEL, 1)], axis=0) + far_own[LEAVES]
    parent = stacked(parent[:, :SKEL])
    handed = folded(mul(parent, th[...]) + mul(parent, tl[...]))
    for m in range(4):
        down = handed[:, m * 128:(m + 1) * 128]
        even = far_sum[pl.ds(2 * m, 4, stride=8), :]
        odd = far_sum[pl.ds(2 * m + 1, 4, stride=8), :]
        even = jnp.concatenate([even, pltpu.roll(even, SKEL, 1)], axis=0) + far_own[2 * m] + down
        odd = jnp.concatenate([pltpu.roll(odd, SKEL, 1), odd], axis=0) + far_own[2 * m + 1] + down
        zero = jnp.zeros_like(even)
        both = jnp.concatenate([stacked(jnp.where(left, even, zero)), stacked(jnp.where(left, zero, odd))], axis=0)
        got = mul(both, ih[m]) + mul(both, il[m])
        for u in range(2):
            own_sum[2 * m + u] = own_sum[2 * m + u] + folded(got[16 * u:16 * u + 16])

    for g in AWAY:
        reply_copy(g, 1).wait_recv()
    for leaf in range(LEAVES):
        total = own_sum[leaf]
        for g in AWAY:
            total = total + near_recv[g, leaf]
        out[:, leaf * LEAF:(leaf + 1) * LEAF] = COUPLE * total


    for copy in mix_copies + data_copies + skel_copies + part_copies:
        copy.wait_send()
    for j in range(1, sides):
        interp_copy(j).wait_send()
    for g in AWAY:
        step = ORDER[g] - REACH
        table_copy(g, step).wait_send()
        reply_copy(g, step).wait_send()
        far_copy(ORDER[g]).wait_send()


def shards(
    leaf_coords, charges, leaf_skeleton, parent_skeleton, interp, transfer,
    near_offset, near_partner, near_count, far_offset, far_partner,
):
    boxes, sides = lax.axis_size("box"), lax.axis_size("rhs")
    V, S, M = pltpu.VMEM, pltpu.SemaphoreType.DMA, pltpu.SMEM
    operands = (
        leaf_coords, charges, leaf_skeleton, parent_skeleton, interp, transfer,
        near_offset.reshape(1, -1), near_partner, near_count, far_offset.reshape(1, -1), far_partner,
    )
    return pl.pallas_call(
        functools.partial(kernel, boxes, sides),
        out_shape=jax.ShapeDtypeStruct(charges.shape, f32),
        in_specs=[pl.BlockSpec(memory_space=pltpu.HBM)] * len(operands),
        out_specs=pl.BlockSpec(memory_space=pltpu.VMEM),
        scratch_shapes=[
            V((SPAN, LEAVES, COLS, LEAF), f32),
            V((SPAN, LEAVES, 3, LEAF), f32),
            V((SPAN * LEAVES, COLS, LEAF), f32),
            V((SPAN * LEAVES, 3, LEAF), f32),
            V((4, COLS, 2 * LEAF), f32),
            V((4, COLS, 256), f32),
            V((32, 256), f32),
            V((SKEL, 512), bf16),
            V((SKEL, 512), bf16),
        ]
        + [V(a.shape, f32) for a in (charges, leaf_coords, leaf_skeleton, parent_skeleton, transfer)]
        + [M(a.shape, i32) for a in operands[6:]]
        + [
            V((8, 128), i32),
            M((8, 128), i32),
            V((SPAN, 3, TABLE), f32),
            V((SPAN, COLS, TABLE), f32),
            V((SPAN, LEAVES, COLS, LEAF), f32),
            V((SPAN, LEAVES, COLS, LEAF), f32),
            V((SPAN, 8, TABLE), f32),
            V((SPAN, 8, TABLE), f32),
            V((4, 2, SKEL, LEAF), f32),
            V((3, LEAVES, LEAF, 128), f32),
            V((3, ENTRIES * SKEL, 128), f32),
            V((LEAVES, 16, LEAF), bf16),
            V((LEAF, LEAF), bf16),
            V((LEAF, LEAF), bf16),
            V((LEAF, LEAF), bf16),
            V((LEAF, LEAF), bf16),
            V((NEAR_ROWS, COLS, LEAF), f32),
            V((NEAR_ROWS, COLS, LEAF), f32),
            V((LEAVES, COLS, LEAF), f32),
            V((128, 128), bf16),
            V((64, 16, 128), f32),
            V((64, 16, 128), f32),
            V((3, 128, FAR_PER * SKEL), bf16),
            V((3, 16, FAR_PER * SKEL), bf16),
            V((512, 128), f32),
            V((ENTRIES, 8, 128), f32),
            V((128, 1024), bf16),
            V((4, 128, LEAF), bf16),
            V((4, 128, LEAF), bf16),
            V((32, 128), f32),
            S((11,)), S(()), S((3,)), S((3,)), S((3,)), S((3,)), S((3,)), S((3,)), S((3, SPAN)), S((3, SPAN)), S((SPAN,)), S((SPAN,)),
            S((SPAN,)), S((SPAN,)), S((SPAN,)), S((SPAN,)),
        ],
        compiler_params=pltpu.CompilerParams(
            collective_id=0, has_side_effects=True, vmem_limit_bytes=60 * 2**20
        ),
    )(*operands)


def solution(mesh):
    return jax.shard_map(
        shards,
        mesh=mesh,
        in_specs=(
            P(None, "box"),
            P("rhs", "box"),
            P(None, "box"),
            P(None, "box"),
            P(("box", "rhs"), None, None),
            P("box", None, None),
            P(),
            P(),
            P(),
            P(),
            P(),
        ),
        out_specs=P("rhs", "box"),
        check_vma=False,
    )
```

```python
import functools

import jax
import jax.numpy as jnp
from jax import lax
from jax.experimental import pallas as pl
from jax.experimental.pallas import tpu as pltpu
from jax.sharding import PartitionSpec as P

REACH = 3
SPAN = 2 * REACH + 1
HOME = 3
FIRST = (1, 2, 3, 0, -1, -2, -3)
USUAL = (1, 3, -3, 0, 2, -2, -1)
SENDS = (4, 6, 0, 5, 1, 2)
SOFTEN = 0.0025
COUPLE = 0.07957747154594767

LEAF = 256
SKEL = 64
LEAVES = 8
COLS = 8
NEAR_PER = 10
FAR_PER = 12
ENTRIES = 9
NEAR_ROWS = LEAVES * NEAR_PER
FAR_ROWS = ENTRIES * FAR_PER
TABLE = 640

MESH = pl.DeviceIdType.MESH
NN = (((1,), (0,)), ((), ()))
NT = (((1,), (1,)), ((), ()))
f32, bf16, i32 = jnp.float32, jnp.bfloat16, jnp.int32


def split(value):
    high = value.astype(bf16)
    low = (value - high.astype(f32)).astype(bf16)
    return high, low


def stacked(value):
    return jnp.concatenate(split(value), axis=0)


def folded(value):
    return value[:8] + value[8:16]


def mul(a, b, dims=NN):
    return lax.dot_general(a, b, dims, preferred_element_type=f32)


def lane_index(shape):
    return lax.broadcasted_iota(i32, shape, 1)


def row_index(shape):
    return lax.broadcasted_iota(i32, shape, 0)


def column_form(row, width):
    return jnp.transpose(jnp.broadcast_to(row, (128, width)))


def inverse_distance(ax, ay, az, bx, by, bz):
    dx, dy, dz = ax - bx, ay - by, az - bz
    return lax.rsqrt((dx * dx + SOFTEN) + (dy * dy + dz * dz))


def tile_pieces(spread, leaf, points, high, low):
    def piece(c):
        s = pl.ds(c * 32, 32)
        for h in range(2):
            at = slice(h * 128, h * 128 + 128)
            k = inverse_distance(
                spread[0, leaf, s, :], spread[1, leaf, s, :], spread[2, leaf, s, :],
                points[0:1, at], points[1:2, at], points[2:3, at],
            )
            high[s, at], low[s, at] = split(k)

    return [functools.partial(piece, c) for c in range(8)]


def interleave(first, second):
    each = max(1, -(-len(second) // max(1, len(first))))
    for j, step in enumerate(first):
        step()
        for other in second[j * each:(j + 1) * each]:
            other()
    for other in second[len(first) * each:]:
        other()


def kernel(
    boxes, sides,
    coords, charges, leaf_skel, parent_skel, interp, transfer,
    near_offset, near_partner, near_count, far_offset, far_partner,
    out,
    vals_in, pts_in, vals, pts, mixed, parts, part_send, th, tl,
    charges_v, coords_v, leaf_skel_v, parent_skel_v, transfer_v,
    noff, npart, ncount, foff, fpart, plan_v, plan,
    skel, tables, near_send, near_recv, far_send, far_recv, gathered,
    spread, spread_skel, own_v, kh0, kh1, kl0, kl1, near_run, near_own, own_sum, chosen_far,
    left_t, right_t, k_far, v_far, far_x, far_own, far_mat, ih, il, far_sum,
    s_load, s_plan, s_mix, r_mix, s_part, r_part, s_int, r_int, s_dat, r_dat, s_tab, r_tab, s_near, r_near, s_far, r_far,
):
    me = lax.axis_index("box")
    side = lax.axis_index("rhs")
    others = [o for o in range(SPAN) if o != REACH]

    ends = (me < REACH) | (me >= boxes - REACH)
    steps = [jnp.where(ends, FIRST[g], USUAL[g]) for g in range(SPAN)]

    def step_from(g, t):
        return jnp.where(t == 0, steps[g], jnp.where(t == 1, steps[g + 1], steps[g + 2]))

    def box_at(step):
        return lax.rem(me + (step + boxes), boxes)

    def side_at(step):
        return lax.rem(side + step, sides)

    barrier = pltpu.get_barrier_semaphore()
    for o in others:
        pl.semaphore_signal(barrier, inc=1, device_id={"box": box_at(o - REACH)}, device_id_type=MESH)
    for j in range(1, sides):
        pl.semaphore_signal(barrier, inc=1, device_id={"rhs": side_at(j)}, device_id_type=MESH)

    loads = []
    for src, dst in (
        (charges, charges_v), (coords, coords_v), (leaf_skel, leaf_skel_v), (parent_skel, parent_skel_v),
        (near_offset, noff), (near_partner, npart), (near_count, ncount),
        (far_offset, foff), (far_partner, fpart), (interp, gathered.at[side]), (transfer, transfer_v),
    ):
        copy = pltpu.make_async_copy(src, dst, s_load.at[len(loads)])
        copy.start()
        loads.append(copy)

    for copy in loads[:4]:
        copy.wait()
    for leaf in range(LEAVES):
        at = slice(leaf * LEAF, (leaf + 1) * LEAF)
        vals_in[REACH, leaf] = charges_v[:, at]
        pts_in[REACH, leaf] = coords_v[:, at]
        vals[HOME * LEAVES + leaf] = charges_v[:, at]
        pts[HOME * LEAVES + leaf] = coords_v[:, at]
    skel[REACH, :, :512] = leaf_skel_v[...]
    skel[REACH, :, 512:] = jnp.concatenate([parent_skel_v[...], parent_skel_v[...]], axis=1)

    def remote(src, dst, send, recv, device):
        copy = pltpu.make_async_remote_copy(
            src_ref=src, dst_ref=dst, send_sem=send, recv_sem=recv, device_id=device, device_id_type=MESH
        )
        copy.start()
        return copy

    pl.semaphore_wait(barrier, len(others) + sides - 1)
    two = 2 * LEAF
    mix_copies = [
        remote(
            charges_v.at[:, pl.ds(pl.multiple_of(side_at(j) * two, two), two)], mixed.at[side],
            s_mix.at[j - 1], r_mix.at[j - 1], {"rhs": side_at(j)},
        )
        for j in range(1, sides)
    ]

    def data_copy(n, o, target):
        src = (vals_in, pts_in)[n]
        return pltpu.make_async_remote_copy(
            src_ref=src.at[REACH], dst_ref=src.at[o], send_sem=s_dat.at[n, o], recv_sem=r_dat.at[n, o],
            device_id=target, device_id_type=MESH,
        )

    data_copies, skel_copies = [], []
    for o in SENDS:
        target = {"box": box_at(REACH - o)}
        for n in range(2):
            copy = data_copy(n, o, target)
            copy.start()
            data_copies.append(copy)
    for o in others:
        target = {"box": box_at(REACH - o)}
        skel_copies.append(remote(skel.at[REACH], skel.at[o], s_dat.at[2, o], r_dat.at[2, o], target))

    for leaf in range(LEAVES):
        at = slice(leaf * LEAF, (leaf + 1) * LEAF)
        own_v[leaf] = stacked(charges_v[:, at])
        for d in range(3):
            spread[d, leaf] = column_form(coords_v[d:d + 1, at], LEAF)

    for copy in loads[4:9]:
        copy.wait()
    alive = ncount[me]
    near_base, far_base = me * NEAR_ROWS, me * FAR_ROWS
    lanes = lane_index((1, 128))
    code = jnp.full((1, 128), 63 * 8, i32)
    for k in range(NEAR_ROWS):
        one = noff[0, near_base + k] * 64 + npart[near_base + k] * 8 + k // NEAR_PER + jnp.where(k < alive, 512, 0)
        code = jnp.where(lanes == k, one, code)
    offset = (code >> 6) & 7
    group = sum(jnp.where(offset == steps[g] + REACH, g, 0) for g in range(SPAN))
    code = code + jnp.where(offset == SPAN, 0, group - offset) * 64
    code_col = column_form(code, 128)
    pair, pair_col = (code >> 3) & 63, (code_col >> 3) & 63
    key, key_col = pair * 128 + lanes, pair_col * 128 + row_index((128, 128))
    rank = jnp.sum((key_col < key).astype(i32), axis=0, keepdims=True)
    placed = column_form(rank, 128) == lanes
    code = jnp.sum(jnp.where(placed, code_col, 0), axis=0, keepdims=True)
    before = pltpu.roll(jnp.broadcast_to(code, (8, 128)), 1, 1)[0:1]
    same = (lanes > 0) & ((code >> 3) & 63 == (before >> 3) & 63)
    upto = jnp.sum((pair_col <= lanes).astype(i32), axis=0, keepdims=True)
    named = jnp.sum((pair_col == lanes).astype(i32), axis=0, keepdims=True)
    plan_v[0:1, :] = code + jnp.where(same, 1024, 0)
    plan_v[1:2, :] = jnp.where(named > 0, upto, 0)
    plan_v[2:3, :] = rank
    plan_v[3:8, :] = jnp.zeros((5, 128), i32)
    plan_copy = pltpu.make_async_copy(plan_v, plan, s_plan)
    plan_copy.start()

    left = lane_index((8, 128)) < SKEL
    for copy in loads[9:]:
        copy.wait()
    mixed[side] = charges_v[:, pl.ds(pl.multiple_of(side * two, two), two)]
    for copy in mix_copies:
        copy.wait_recv()
    high, low = split(gathered[side].reshape(128, LEAF))
    columns = [
        jnp.concatenate([mixed[q, :, u * LEAF:(u + 1) * LEAF] for q in range(4)], axis=0) for u in range(2)
    ]
    both = jnp.concatenate([stacked(columns[0]), stacked(columns[1])], axis=0)
    got = mul(both, high, NT) + mul(both, low, NT)
    weights = jnp.where(
        lane_index((32, 128)) < SKEL, got[0:32] + got[32:64], got[64:96] + got[96:128]
    )
    high, low = split(transfer_v[0, :, pl.ds(pl.multiple_of(side * 128, 128), 128)])
    both = stacked(weights)
    got = mul(both, high, NT) + mul(both, low, NT)
    got = got[:32] + got[32:]
    part_send[:, 0:128] = weights
    part_send[:, 128:256] = jnp.concatenate([got, got], axis=1)
    part_copies = [
        remote(
            part_send.at[pl.ds(pl.multiple_of(side_at(j) * 8, 8), 8)], parts.at[side],
            s_part.at[j - 1], r_part.at[j - 1], {"rhs": side_at(j)},
        )
        for j in range(1, sides)
    ]
    parts[side] = part_send[pl.ds(pl.multiple_of(side * 8, 8), 8), :]
    th[...], tl[...] = split(transfer_v[0])

    buffers = ((kh0, kl0), (kh1, kl1))

    def self_pair(t, carry):
        for u in range(2):
            leaf = t * 2 + u
            for step in tile_pieces(spread, leaf, pts[HOME * LEAVES + leaf], *buffers[u]):
                step()
        for u in range(2):
            leaf = t * 2 + u
            high, low = buffers[u]
            v = own_v[leaf]
            own_sum[leaf] = folded(mul(v, high[...], NT) + mul(v, low[...], NT))
        return carry

    lax.fori_loop(0, LEAVES // 2, self_pair, 0)

    for d in range(3):
        spread_skel[d, :LEAVES * SKEL] = column_form(leaf_skel_v[d:d + 1, :], LEAVES * SKEL)
        spread_skel[d, LEAVES * SKEL:] = column_form(parent_skel_v[d:d + 1, :], SKEL)
    near_run[...] = jnp.zeros_like(near_run)
    pairs = FAR_ROWS // 2
    far_x[pairs * 8:, :] = jnp.zeros((512 - pairs * 8, 128), f32)
    for u in range(2):
        key_row = jnp.full((1, 128), -1, i32)
        for j in range(pairs):
            o, p = foff[0, far_base + 2 * j + u], fpart[far_base + 2 * j + u]
            key = jnp.where(p < LEAVES, o * 8 + p, 8 * SPAN + o)
            key_row = jnp.where((lanes == j) | (lanes == j + 64), key, key_row)
        chosen_far[u * 64:(u + 1) * 64, :] = jnp.where(row_index((64, 128)) == key_row, 1.0, 0.0).astype(bf16)

    plan_copy.wait()

    def arrive(g, step):
        o = step + REACH
        for n in range(2):
            data_copy(n, o, {"box": box_at(1)}).wait_recv()
        for leaf in range(LEAVES):
            vals[g * LEAVES + leaf] = vals_in[o, leaf]
            pts[g * LEAVES + leaf] = pts_in[o, leaf]

    def table_copy(g, step):
        slot = step + REACH
        return pltpu.make_async_remote_copy(
            src_ref=tables.at[REACH], dst_ref=tables.at[slot], send_sem=s_tab.at[slot], recv_sem=r_tab.at[slot],
            device_id={"box": box_at(-step)}, device_id_type=MESH,
        )

    def reply_copy(g, step):
        o = step + REACH
        return pltpu.make_async_remote_copy(
            src_ref=near_send.at[g], dst_ref=near_recv.at[o], send_sem=s_near.at[o], recv_sem=r_near.at[o],
            device_id={"box": box_at(step)}, device_id_type=MESH,
        )

    def interp_copy(j):
        return pltpu.make_async_remote_copy(
            src_ref=interp, dst_ref=gathered.at[side], send_sem=s_int.at[j - 1], recv_sem=r_int.at[j - 1],
            device_id={"rhs": side_at(j)}, device_id_type=MESH,
        )

    def far_copy(o):
        return pltpu.make_async_remote_copy(
            src_ref=far_send.at[o], dst_ref=far_recv.at[o], send_sem=s_far.at[o], recv_sem=r_far.at[o],
            device_id={"box": box_at(o - REACH)}, device_id_type=MESH,
        )

    def near_reply(g):
        for p in range(LEAVES):
            last = plan[1, g * 8 + p]
            some = jnp.where(last > 0, 1.0, 0.0).astype(f32)
            near_send[g, p] = near_run[jnp.maximum(last - 1, 0)] * some

    def near_phase(t, run):
        @pl.when(t > 1)
        def _():
            arrive(t + 2, step_from(4, t - 2))

        first = t * 16
        kept_run = [run]

        def tile(u):
            code = plan[0, first + u]
            return tile_pieces(spread, code & 7, pts[(code >> 3) & 63], *buffers[u % 2])

        def matmuls(u):
            high, low = buffers[u % 2]
            code = plan[0, first + u]
            kept = {}

            def start():
                kept["live"] = ((code >> 9) & 1).astype(f32)
                kept["v"] = stacked(vals[(code >> 3) & 63] * kept["live"])
                kept["own"] = mul(kept["v"], high[...], NT)

            def second():
                near_own[first + u] = folded(kept["own"] + mul(kept["v"], low[...], NT))

            def third():
                kept["own_v"] = own_v[code & 7]
                kept["other"] = mul(kept["own_v"], high[...])

            def fourth():
                other = folded(kept["other"] + mul(kept["own_v"], low[...]))
                again = ((code >> 10) & 1).astype(f32)
                kept_run[0] = kept_run[0] * again + other * kept["live"]
                near_run[first + u] = kept_run[0]

            return [start, second, third, fourth]

        for step in tile(0):
            step()
        for u in range(16):
            interleave(matmuls(u), tile(u + 1) if u + 1 < 16 else [])

        @pl.when(t < 3)
        def _():
            near_reply(t)
            reply_copy(t, step_from(0, t)).start()

        @pl.when((t == 0) & (me < REACH))
        def _():
            send_table()

        @pl.when(t == 4)
        def _():
            for g in (4, 5, 6):
                near_reply(g)
                reply_copy(g, steps[g]).start()

        @pl.when(t == 2)
        def _():
            far_pairs()

        return kept_run[0]

    def send_table():
        for copy in part_copies:
            copy.wait_recv()
        total = parts[0, :, 128:256]
        for m in range(4):
            tables[REACH, :, m * 128:(m + 1) * 128] = parts[m, :, 0:128]
            if m:
                total = total + parts[m, :, 128:256]
        tables[REACH, :, 512:640] = total
        for o in SENDS:
            table_copy(0, o - REACH).start()
        for j in range(1, sides):
            interp_copy(j).start()

    def far_pairs():
        for copy in skel_copies:
            copy.wait_recv()
        for o in others:
            table_copy(0, o - REACH).wait_recv()
        left3 = lane_index((3, 128)) < SKEL

        def halves(block, mask):
            turned = pltpu.roll(block, SKEL, 1)
            zero = jnp.zeros_like(block)
            even = (jnp.where(mask, block, zero), jnp.where(mask, zero, turned))
            odd = (jnp.where(mask, turned, zero), jnp.where(mask, zero, block))
            return even, odd

        def put(slot, value_pair, point_pair):
            for table, value, point in zip((left_t, right_t), value_pair, point_pair):
                table[slot, 0:8, :] = value
                table[slot, 8:11, :] = point

        for o in range(SPAN):
            for m in range(4):
                at = slice(m * 128, (m + 1) * 128)
                values = halves(tables[o, :, at], left)
                points = halves(skel[o, :, at], left3)
                for u in range(2):
                    put(o * ENTRIES + 2 * m + u, values[u], points[u])
            values = halves(tables[o, :, 512:640], left)
            points = halves(skel[o, :, 512:640], left3)
            put(o * ENTRIES + LEAVES, values[0], points[0])

        def far_slot(k):
            return foff[0, far_base + k] * ENTRIES + fpart[far_base + k]

        def far_three(t, carry):
            def tiles(u):
                e = t * 3 + u
                rows = pl.ds(pl.multiple_of(e * SKEL, SKEL), SKEL)
                for j in range(FAR_PER // 2):
                    at = slice(j * 128, (j + 1) * 128)
                    k = e * FAR_PER + 2 * j
                    block = left_t[far_slot(k), 0:11, :] + right_t[far_slot(k + 1), 0:11, :]
                    tile = inverse_distance(
                        spread_skel[0, rows, :], spread_skel[1, rows, :], spread_skel[2, rows, :],
                        block[8:9], block[9:10], block[10:11],
                    )
                    k_far[u, 0:SKEL, at], k_far[u, SKEL:, at] = split(tile)
                    v_far[u, :, at] = stacked(block[0:8])

            def matmuls(u):
                e = t * 3 + u
                mine = left_t[REACH * ENTRIES + e, 0:8, :] + right_t[REACH * ENTRIES + e, 0:8, :]
                every = k_far[u]
                other = folded(mul(stacked(mine), every))
                for j in range(FAR_PER // 2):
                    at = pl.ds(pl.multiple_of((e * (FAR_PER // 2) + j) * 8, 8), 8)
                    far_x[at, :] = other[:, j * 128:(j + 1) * 128]
                own = folded(mul(v_far[u], every, NT))
                far_own[e] = own + pltpu.roll(own, SKEL, 1)

            tiles(0)
            tiles(1)
            matmuls(0)
            tiles(2)
            matmuls(1)
            matmuls(2)
            return carry

        lax.fori_loop(0, ENTRIES // 3, far_three, 0)

        for r in range(COLS):
            high, low = split(far_x[pl.ds(r, 64, stride=8), :])
            far_mat[0:64, r * 128:(r + 1) * 128] = high
            far_mat[64:128, r * 128:(r + 1) * 128] = low
        reply = mul(chosen_far[...], far_mat[...])
        left64 = lane_index((64, 128)) < SKEL
        for m in range(4):
            a, b = slice(m * 128, (m + 1) * 128), slice((m + 4) * 128, (m + 5) * 128)
            straight = jnp.where(left64, reply[:64, a], reply[64:, b])
            crossed = jnp.where(left64, reply[:64, b], reply[64:, a])
            whole = straight + pltpu.roll(crossed, SKEL, 1)
            for o in range(SPAN):
                far_send[o, :, a] = whole[8 * o:8 * o + 8]
                far_send[o, m:m + 1, 512:640] = whole[8 * SPAN + o:8 * SPAN + o + 1]
        for o in range(SPAN):
            far_send[o, 4:8, 512:640] = jnp.zeros((4, 128), f32)
        for o in (4, 5, 6, 2, 1, 0):
            far_copy(o).start()

    @pl.when(me >= REACH)
    def _():
        send_table()

    for g in range(3):
        arrive(g, steps[g])
    lax.fori_loop(0, 5, near_phase, jnp.zeros((COLS, LEAF), f32))
    near_reply(HOME)

    for leaf in range(LEAVES):
        total = own_sum[leaf] + near_send[HOME, leaf]
        for u in range(NEAR_PER):
            total = total + near_own[plan[2, leaf * NEAR_PER + u]]
        own_sum[leaf] = total
    for j in range(1, sides):
        interp_copy(j).wait_recv()
    for m in range(4):
        ih[m], il[m] = split(gathered[m].reshape(128, LEAF))
    for o in others:
        far_copy(o).wait_recv()
    total = far_send[REACH]
    for o in others:
        total = total + far_recv[o]
    for m in range(4):
        far_sum[m * 8:(m + 1) * 8, :] = total[:, m * 128:(m + 1) * 128]
    fours = total[0:4, 512:640]
    parent = jnp.concatenate([fours, pltpu.roll(fours, SKEL, 1)], axis=0) + far_own[LEAVES]
    parent = stacked(parent[:, :SKEL])
    handed = folded(mul(parent, th[...]) + mul(parent, tl[...]))
    for m in range(4):
        down = handed[:, m * 128:(m + 1) * 128]
        even = far_sum[pl.ds(2 * m, 4, stride=8), :]
        odd = far_sum[pl.ds(2 * m + 1, 4, stride=8), :]
        even = jnp.concatenate([even, pltpu.roll(even, SKEL, 1)], axis=0) + far_own[2 * m] + down
        odd = jnp.concatenate([pltpu.roll(odd, SKEL, 1), odd], axis=0) + far_own[2 * m + 1] + down
        zero = jnp.zeros_like(even)
        both = jnp.concatenate([stacked(jnp.where(left, even, zero)), stacked(jnp.where(left, zero, odd))], axis=0)
        got = mul(both, ih[m]) + mul(both, il[m])
        for u in range(2):
            own_sum[2 * m + u] = own_sum[2 * m + u] + folded(got[16 * u:16 * u + 16])

    for o in others:
        reply_copy(0, o - REACH).wait_recv()
    for leaf in range(LEAVES):
        total = own_sum[leaf]
        for o in others:
            total = total + near_recv[o, leaf]
        out[:, leaf * LEAF:(leaf + 1) * LEAF] = COUPLE * total


    for copy in mix_copies + data_copies + skel_copies + part_copies:
        copy.wait_send()
    for j in range(1, sides):
        interp_copy(j).wait_send()
    for o in others:
        table_copy(0, o - REACH).wait_send()
        reply_copy(0, o - REACH).wait_send()
        far_copy(o).wait_send()


def shards(
    leaf_coords, charges, leaf_skeleton, parent_skeleton, interp, transfer,
    near_offset, near_partner, near_count, far_offset, far_partner,
):
    boxes, sides = lax.axis_size("box"), lax.axis_size("rhs")
    V, S, M = pltpu.VMEM, pltpu.SemaphoreType.DMA, pltpu.SMEM
    operands = (
        leaf_coords, charges, leaf_skeleton, parent_skeleton, interp, transfer,
        near_offset.reshape(1, -1), near_partner, near_count, far_offset.reshape(1, -1), far_partner,
    )
    return pl.pallas_call(
        functools.partial(kernel, boxes, sides),
        out_shape=jax.ShapeDtypeStruct(charges.shape, f32),
        in_specs=[pl.BlockSpec(memory_space=pltpu.HBM)] * len(operands),
        out_specs=pl.BlockSpec(memory_space=pltpu.VMEM),
        scratch_shapes=[
            V((SPAN, LEAVES, COLS, LEAF), f32),
            V((SPAN, LEAVES, 3, LEAF), f32),
            V((SPAN * LEAVES, COLS, LEAF), f32),
            V((SPAN * LEAVES, 3, LEAF), f32),
            V((4, COLS, 2 * LEAF), f32),
            V((4, COLS, 256), f32),
            V((32, 256), f32),
            V((SKEL, 512), bf16),
            V((SKEL, 512), bf16),
        ]
        + [V(a.shape, f32) for a in (charges, leaf_coords, leaf_skeleton, parent_skeleton, transfer)]
        + [M(a.shape, i32) for a in operands[6:]]
        + [
            V((8, 128), i32),
            M((8, 128), i32),
            V((SPAN, 3, TABLE), f32),
            V((SPAN, COLS, TABLE), f32),
            V((SPAN, LEAVES, COLS, LEAF), f32),
            V((SPAN, LEAVES, COLS, LEAF), f32),
            V((SPAN, 8, TABLE), f32),
            V((SPAN, 8, TABLE), f32),
            V((4, 2, SKEL, LEAF), f32),
            V((3, LEAVES, LEAF, 128), f32),
            V((3, ENTRIES * SKEL, 128), f32),
            V((LEAVES, 16, LEAF), bf16),
            V((LEAF, LEAF), bf16),
            V((LEAF, LEAF), bf16),
            V((LEAF, LEAF), bf16),
            V((LEAF, LEAF), bf16),
            V((NEAR_ROWS, COLS, LEAF), f32),
            V((NEAR_ROWS, COLS, LEAF), f32),
            V((LEAVES, COLS, LEAF), f32),
            V((128, 128), bf16),
            V((64, 16, 128), f32),
            V((64, 16, 128), f32),
            V((3, 128, FAR_PER * SKEL), bf16),
            V((3, 16, FAR_PER * SKEL), bf16),
            V((512, 128), f32),
            V((ENTRIES, 8, 128), f32),
            V((128, 1024), bf16),
            V((4, 128, LEAF), bf16),
            V((4, 128, LEAF), bf16),
            V((32, 128), f32),
            S((11,)), S(()), S((3,)), S((3,)), S((3,)), S((3,)), S((3,)), S((3,)), S((3, SPAN)), S((3, SPAN)), S((SPAN,)), S((SPAN,)),
            S((SPAN,)), S((SPAN,)), S((SPAN,)), S((SPAN,)),
        ],
        compiler_params=pltpu.CompilerParams(
            collective_id=0, has_side_effects=True, vmem_limit_bytes=60 * 2**20
        ),
    )(*operands)


def solution(mesh):
    return jax.shard_map(
        shards,
        mesh=mesh,
        in_specs=(
            P(None, "box"),
            P("rhs", "box"),
            P(None, "box"),
            P(None, "box"),
            P(("box", "rhs"), None, None),
            P("box", None, None),
            P(),
            P(),
            P(),
            P(),
            P(),
        ),
        out_specs=P("rhs", "box"),
        check_vma=False,
    )
```

```python
import functools

import jax
import jax.numpy as jnp
from jax import lax
from jax.experimental import pallas as pl
from jax.experimental.pallas import tpu as pltpu
from jax.sharding import PartitionSpec as P

REACH = 3
SPAN = 2 * REACH + 1
HOME = 3
FIRST = (1, 2, 3, 0, -1, -2, -3)
USUAL = (1, 3, -3, 0, 2, -2, -1)
SENDS = (4, 6, 0, 5, 1, 2)
SOFTEN = 0.0025
COUPLE = 0.07957747154594767

LEAF = 256
SKEL = 64
LEAVES = 8
COLS = 8
NEAR_PER = 10
FAR_PER = 12
ENTRIES = 9
NEAR_ROWS = LEAVES * NEAR_PER
FAR_ROWS = ENTRIES * FAR_PER
TABLE = 640

MESH = pl.DeviceIdType.MESH
NN = (((1,), (0,)), ((), ()))
NT = (((1,), (1,)), ((), ()))
f32, bf16, i32 = jnp.float32, jnp.bfloat16, jnp.int32


def split(value):
    high = value.astype(bf16)
    low = (value - high.astype(f32)).astype(bf16)
    return high, low


def stacked(value):
    return jnp.concatenate(split(value), axis=0)


def folded(value):
    return value[:8] + value[8:16]


def mul(a, b, dims=NN):
    return lax.dot_general(a, b, dims, preferred_element_type=f32)


def lane_index(shape):
    return lax.broadcasted_iota(i32, shape, 1)


def row_index(shape):
    return lax.broadcasted_iota(i32, shape, 0)


def column_form(row, width):
    return jnp.transpose(jnp.broadcast_to(row, (128, width)))


def inverse_distance(ax, ay, az, bx, by, bz):
    dx, dy, dz = ax - bx, ay - by, az - bz
    return lax.rsqrt((dx * dx + SOFTEN) + (dy * dy + dz * dz))


def tile_pieces(spread, leaf, points, high, low):
    def piece(c):
        s = pl.ds(c * 32, 32)
        for h in range(2):
            at = slice(h * 128, h * 128 + 128)
            k = inverse_distance(
                spread[0, leaf, s, :], spread[1, leaf, s, :], spread[2, leaf, s, :],
                points[0:1, at], points[1:2, at], points[2:3, at],
            )
            high[s, at], low[s, at] = split(k)

    return [functools.partial(piece, c) for c in range(8)]


def interleave(first, second):
    each = max(1, -(-len(second) // max(1, len(first))))
    for j, step in enumerate(first):
        step()
        for other in second[j * each:(j + 1) * each]:
            other()
    for other in second[len(first) * each:]:
        other()


def kernel(
    boxes, sides,
    coords, charges, leaf_skel, parent_skel, interp, transfer,
    near_offset, near_partner, near_count, far_offset, far_partner,
    out,
    vals_in, pts_in, vals, pts, mixed, parts, part_send, th, tl,
    charges_v, coords_v, leaf_skel_v, parent_skel_v, transfer_v,
    noff, npart, ncount, foff, fpart, plan_v, plan,
    skel, tables, near_send, near_recv, far_send, far_recv, gathered,
    spread, spread_skel, own_v, kh0, kh1, kl0, kl1, near_run, near_own, own_sum, chosen_far,
    left_t, right_t, k_far, v_far, far_x, far_own, far_mat, ih, il, far_sum,
    s_load, s_plan, s_mix, r_mix, s_part, r_part, s_int, r_int, s_dat, r_dat, s_tab, r_tab, s_near, r_near, s_far, r_far,
):
    me = lax.axis_index("box")
    side = lax.axis_index("rhs")
    others = [o for o in range(SPAN) if o != REACH]

    ends = (me < REACH) | (me >= boxes - REACH)
    steps = [jnp.where(ends, FIRST[g], USUAL[g]) for g in range(SPAN)]

    def step_from(g, t):
        return jnp.where(t == 0, steps[g], jnp.where(t == 1, steps[g + 1], steps[g + 2]))

    def box_at(step):
        return lax.rem(me + (step + boxes), boxes)

    def side_at(step):
        return lax.rem(side + step, sides)

    barrier = pltpu.get_barrier_semaphore()
    for o in others:
        pl.semaphore_signal(barrier, inc=1, device_id={"box": box_at(o - REACH)}, device_id_type=MESH)
    for j in range(1, sides):
        pl.semaphore_signal(barrier, inc=1, device_id={"rhs": side_at(j)}, device_id_type=MESH)

    loads = []
    for src, dst in (
        (charges, charges_v), (coords, coords_v), (leaf_skel, leaf_skel_v), (parent_skel, parent_skel_v),
        (near_offset, noff), (near_partner, npart), (near_count, ncount),
        (far_offset, foff), (far_partner, fpart), (interp, gathered.at[side]), (transfer, transfer_v),
    ):
        copy = pltpu.make_async_copy(src, dst, s_load.at[len(loads)])
        copy.start()
        loads.append(copy)

    for copy in loads[:4]:
        copy.wait()
    for leaf in range(LEAVES):
        at = slice(leaf * LEAF, (leaf + 1) * LEAF)
        vals_in[REACH, leaf] = charges_v[:, at]
        pts_in[REACH, leaf] = coords_v[:, at]
        vals[HOME * LEAVES + leaf] = charges_v[:, at]
        pts[HOME * LEAVES + leaf] = coords_v[:, at]
    skel[REACH, :, :512] = leaf_skel_v[...]
    skel[REACH, :, 512:] = jnp.concatenate([parent_skel_v[...], parent_skel_v[...]], axis=1)

    def remote(src, dst, send, recv, device):
        copy = pltpu.make_async_remote_copy(
            src_ref=src, dst_ref=dst, send_sem=send, recv_sem=recv, device_id=device, device_id_type=MESH
        )
        copy.start()
        return copy

    pl.semaphore_wait(barrier, len(others) + sides - 1)
    two = 2 * LEAF
    mix_copies = [
        remote(
            charges_v.at[:, pl.ds(pl.multiple_of(side_at(j) * two, two), two)], mixed.at[side],
            s_mix.at[j - 1], r_mix.at[j - 1], {"rhs": side_at(j)},
        )
        for j in range(1, sides)
    ]

    def data_copy(n, o, target):
        src = (vals_in, pts_in)[n]
        return pltpu.make_async_remote_copy(
            src_ref=src.at[REACH], dst_ref=src.at[o], send_sem=s_dat.at[n, o], recv_sem=r_dat.at[n, o],
            device_id=target, device_id_type=MESH,
        )

    data_copies, skel_copies = [], []
    for o in SENDS:
        target = {"box": box_at(REACH - o)}
        for n in range(2):
            copy = data_copy(n, o, target)
            copy.start()
            data_copies.append(copy)
    for o in others:
        target = {"box": box_at(REACH - o)}
        skel_copies.append(remote(skel.at[REACH], skel.at[o], s_dat.at[2, o], r_dat.at[2, o], target))

    for leaf in range(LEAVES):
        at = slice(leaf * LEAF, (leaf + 1) * LEAF)
        own_v[leaf] = stacked(charges_v[:, at])
        for d in range(3):
            spread[d, leaf] = column_form(coords_v[d:d + 1, at], LEAF)

    for copy in loads[4:9]:
        copy.wait()
    alive = ncount[me]
    near_base, far_base = me * NEAR_ROWS, me * FAR_ROWS
    lanes = lane_index((1, 128))
    code = jnp.full((1, 128), 63 * 8, i32)
    for k in range(NEAR_ROWS):
        one = noff[0, near_base + k] * 64 + npart[near_base + k] * 8 + k // NEAR_PER + jnp.where(k < alive, 512, 0)
        code = jnp.where(lanes == k, one, code)
    offset = (code >> 6) & 7
    group = sum(jnp.where(offset == steps[g] + REACH, g, 0) for g in range(SPAN))
    code = code + jnp.where(offset == SPAN, 0, group - offset) * 64
    code_col = column_form(code, 128)
    pair, pair_col = (code >> 3) & 63, (code_col >> 3) & 63
    key, key_col = pair * 128 + lanes, pair_col * 128 + row_index((128, 128))
    rank = jnp.sum((key_col < key).astype(i32), axis=0, keepdims=True)
    placed = column_form(rank, 128) == lanes
    code = jnp.sum(jnp.where(placed, code_col, 0), axis=0, keepdims=True)
    before = pltpu.roll(jnp.broadcast_to(code, (8, 128)), 1, 1)[0:1]
    same = (lanes > 0) & ((code >> 3) & 63 == (before >> 3) & 63)
    upto = jnp.sum((pair_col <= lanes).astype(i32), axis=0, keepdims=True)
    named = jnp.sum((pair_col == lanes).astype(i32), axis=0, keepdims=True)
    plan_v[0:1, :] = code + jnp.where(same, 1024, 0)
    plan_v[1:2, :] = jnp.where(named > 0, upto, 0)
    plan_v[2:3, :] = rank
    plan_v[3:8, :] = jnp.zeros((5, 128), i32)
    plan_copy = pltpu.make_async_copy(plan_v, plan, s_plan)
    plan_copy.start()

    left = lane_index((8, 128)) < SKEL
    for copy in loads[9:]:
        copy.wait()
    mixed[side] = charges_v[:, pl.ds(pl.multiple_of(side * two, two), two)]
    for copy in mix_copies:
        copy.wait_recv()
    high, low = split(gathered[side].reshape(128, LEAF))
    columns = [
        jnp.concatenate([mixed[q, :, u * LEAF:(u + 1) * LEAF] for q in range(4)], axis=0) for u in range(2)
    ]
    both = jnp.concatenate([stacked(columns[0]), stacked(columns[1])], axis=0)
    got = mul(both, high, NT) + mul(both, low, NT)
    weights = jnp.where(
        lane_index((32, 128)) < SKEL, got[0:32] + got[32:64], got[64:96] + got[96:128]
    )
    high, low = split(transfer_v[0, :, pl.ds(pl.multiple_of(side * 128, 128), 128)])
    both = stacked(weights)
    got = mul(both, high, NT) + mul(both, low, NT)
    got = got[:32] + got[32:]
    part_send[:, 0:128] = weights
    part_send[:, 128:256] = jnp.concatenate([got, got], axis=1)
    part_copies = [
        remote(
            part_send.at[pl.ds(pl.multiple_of(side_at(j) * 8, 8), 8)], parts.at[side],
            s_part.at[j - 1], r_part.at[j - 1], {"rhs": side_at(j)},
        )
        for j in range(1, sides)
    ]
    parts[side] = part_send[pl.ds(pl.multiple_of(side * 8, 8), 8), :]
    th[...], tl[...] = split(transfer_v[0])

    buffers = ((kh0, kl0), (kh1, kl1))

    def self_pair(t, carry):
        for u in range(2):
            leaf = t * 2 + u
            for step in tile_pieces(spread, leaf, pts[HOME * LEAVES + leaf], *buffers[u]):
                step()
        for u in range(2):
            leaf = t * 2 + u
            high, low = buffers[u]
            v = own_v[leaf]
            own_sum[leaf] = folded(mul(v, high[...], NT) + mul(v, low[...], NT))
        return carry

    lax.fori_loop(0, LEAVES // 2, self_pair, 0)

    for d in range(3):
        spread_skel[d, :LEAVES * SKEL] = column_form(leaf_skel_v[d:d + 1, :], LEAVES * SKEL)
        spread_skel[d, LEAVES * SKEL:] = column_form(parent_skel_v[d:d + 1, :], SKEL)
    near_run[...] = jnp.zeros_like(near_run)
    pairs = FAR_ROWS // 2
    far_x[pairs * 8:, :] = jnp.zeros((512 - pairs * 8, 128), f32)
    for u in range(2):
        key_row = jnp.full((1, 128), -1, i32)
        for j in range(pairs):
            o, p = foff[0, far_base + 2 * j + u], fpart[far_base + 2 * j + u]
            key = jnp.where(p < LEAVES, o * 8 + p, 8 * SPAN + o)
            key_row = jnp.where((lanes == j) | (lanes == j + 64), key, key_row)
        chosen_far[u * 64:(u + 1) * 64, :] = jnp.where(row_index((64, 128)) == key_row, 1.0, 0.0).astype(bf16)

    plan_copy.wait()

    def arrive(g, step):
        o = step + REACH
        for n in range(2):
            data_copy(n, o, {"box": box_at(1)}).wait_recv()
        for leaf in range(LEAVES):
            vals[g * LEAVES + leaf] = vals_in[o, leaf]
            pts[g * LEAVES + leaf] = pts_in[o, leaf]

    def table_copy(g, step):
        slot = step + REACH
        return pltpu.make_async_remote_copy(
            src_ref=tables.at[REACH], dst_ref=tables.at[slot], send_sem=s_tab.at[slot], recv_sem=r_tab.at[slot],
            device_id={"box": box_at(-step)}, device_id_type=MESH,
        )

    def reply_copy(g, step):
        o = step + REACH
        return pltpu.make_async_remote_copy(
            src_ref=near_send.at[g], dst_ref=near_recv.at[o], send_sem=s_near.at[o], recv_sem=r_near.at[o],
            device_id={"box": box_at(step)}, device_id_type=MESH,
        )

    def interp_copy(j):
        return pltpu.make_async_remote_copy(
            src_ref=interp, dst_ref=gathered.at[side], send_sem=s_int.at[j - 1], recv_sem=r_int.at[j - 1],
            device_id={"rhs": side_at(j)}, device_id_type=MESH,
        )

    def far_copy(o):
        return pltpu.make_async_remote_copy(
            src_ref=far_send.at[o], dst_ref=far_recv.at[o], send_sem=s_far.at[o], recv_sem=r_far.at[o],
            device_id={"box": box_at(o - REACH)}, device_id_type=MESH,
        )

    def near_reply(g):
        for p in range(LEAVES):
            last = plan[1, g * 8 + p]
            some = jnp.where(last > 0, 1.0, 0.0).astype(f32)
            near_send[g, p] = near_run[jnp.maximum(last - 1, 0)] * some

    def near_phase(t, run):
        @pl.when(t > 1)
        def _():
            arrive(t + 2, step_from(4, t - 2))

        first = t * 16
        kept_run = [run]

        def tile(u):
            code = plan[0, first + u]
            return tile_pieces(spread, code & 7, pts[(code >> 3) & 63], *buffers[u % 2])

        def matmuls(u):
            high, low = buffers[u % 2]
            code = plan[0, first + u]
            kept = {}

            def start():
                kept["live"] = ((code >> 9) & 1).astype(f32)
                kept["v"] = stacked(vals[(code >> 3) & 63] * kept["live"])
                kept["own"] = mul(kept["v"], high[...], NT)

            def second():
                near_own[first + u] = folded(kept["own"] + mul(kept["v"], low[...], NT))

            def third():
                kept["own_v"] = own_v[code & 7]
                kept["other"] = mul(kept["own_v"], high[...])

            def fourth():
                other = folded(kept["other"] + mul(kept["own_v"], low[...]))
                again = ((code >> 10) & 1).astype(f32)
                kept_run[0] = kept_run[0] * again + other * kept["live"]
                near_run[first + u] = kept_run[0]

            return [start, second, third, fourth]

        for step in tile(0):
            step()
        for u in range(16):
            interleave(matmuls(u), tile(u + 1) if u + 1 < 16 else [])

        @pl.when(t < 3)
        def _():
            near_reply(t)
            reply_copy(t, step_from(0, t)).start()

        @pl.when((t == 0) & (me < REACH))
        def _():
            send_table()

        @pl.when(t == 4)
        def _():
            for g in (4, 5, 6):
                near_reply(g)
                reply_copy(g, steps[g]).start()

        @pl.when(t == 2)
        def _():
            far_pairs()
            for j in range(1, sides):
                interp_copy(j).start()

        return kept_run[0]

    def send_table():
        for copy in part_copies:
            copy.wait_recv()
        total = parts[0, :, 128:256]
        for m in range(4):
            tables[REACH, :, m * 128:(m + 1) * 128] = parts[m, :, 0:128]
            if m:
                total = total + parts[m, :, 128:256]
        tables[REACH, :, 512:640] = total
        for o in SENDS:
            table_copy(0, o - REACH).start()

    def far_pairs():
        for copy in skel_copies:
            copy.wait_recv()
        for o in others:
            table_copy(0, o - REACH).wait_recv()
        left3 = lane_index((3, 128)) < SKEL

        def halves(block, mask):
            turned = pltpu.roll(block, SKEL, 1)
            zero = jnp.zeros_like(block)
            even = (jnp.where(mask, block, zero), jnp.where(mask, zero, turned))
            odd = (jnp.where(mask, turned, zero), jnp.where(mask, zero, block))
            return even, odd

        def put(slot, value_pair, point_pair):
            for table, value, point in zip((left_t, right_t), value_pair, point_pair):
                table[slot, 0:8, :] = value
                table[slot, 8:11, :] = point

        for o in range(SPAN):
            for m in range(4):
                at = slice(m * 128, (m + 1) * 128)
                values = halves(tables[o, :, at], left)
                points = halves(skel[o, :, at], left3)
                for u in range(2):
                    put(o * ENTRIES + 2 * m + u, values[u], points[u])
            values = halves(tables[o, :, 512:640], left)
            points = halves(skel[o, :, 512:640], left3)
            put(o * ENTRIES + LEAVES, values[0], points[0])

        def far_slot(k):
            return foff[0, far_base + k] * ENTRIES + fpart[far_base + k]

        def far_three(t, carry):
            def tiles(u):
                e = t * 3 + u
                rows = pl.ds(pl.multiple_of(e * SKEL, SKEL), SKEL)
                for j in range(FAR_PER // 2):
                    at = slice(j * 128, (j + 1) * 128)
                    k = e * FAR_PER + 2 * j
                    block = left_t[far_slot(k), 0:11, :] + right_t[far_slot(k + 1), 0:11, :]
                    tile = inverse_distance(
                        spread_skel[0, rows, :], spread_skel[1, rows, :], spread_skel[2, rows, :],
                        block[8:9], block[9:10], block[10:11],
                    )
                    k_far[u, 0:SKEL, at], k_far[u, SKEL:, at] = split(tile)
                    v_far[u, :, at] = stacked(block[0:8])

            def matmuls(u):
                e = t * 3 + u
                mine = left_t[REACH * ENTRIES + e, 0:8, :] + right_t[REACH * ENTRIES + e, 0:8, :]
                every = k_far[u]
                other = folded(mul(stacked(mine), every))
                for j in range(FAR_PER // 2):
                    at = pl.ds(pl.multiple_of((e * (FAR_PER // 2) + j) * 8, 8), 8)
                    far_x[at, :] = other[:, j * 128:(j + 1) * 128]
                own = folded(mul(v_far[u], every, NT))
                far_own[e] = own + pltpu.roll(own, SKEL, 1)

            tiles(0)
            tiles(1)
            matmuls(0)
            tiles(2)
            matmuls(1)
            matmuls(2)
            return carry

        lax.fori_loop(0, ENTRIES // 3, far_three, 0)

        for r in range(COLS):
            high, low = split(far_x[pl.ds(r, 64, stride=8), :])
            far_mat[0:64, r * 128:(r + 1) * 128] = high
            far_mat[64:128, r * 128:(r + 1) * 128] = low
        reply = mul(chosen_far[...], far_mat[...])
        left64 = lane_index((64, 128)) < SKEL
        for m in range(4):
            a, b = slice(m * 128, (m + 1) * 128), slice((m + 4) * 128, (m + 5) * 128)
            straight = jnp.where(left64, reply[:64, a], reply[64:, b])
            crossed = jnp.where(left64, reply[:64, b], reply[64:, a])
            whole = straight + pltpu.roll(crossed, SKEL, 1)
            for o in range(SPAN):
                far_send[o, :, a] = whole[8 * o:8 * o + 8]
                far_send[o, m:m + 1, 512:640] = whole[8 * SPAN + o:8 * SPAN + o + 1]
        for o in range(SPAN):
            far_send[o, 4:8, 512:640] = jnp.zeros((4, 128), f32)
        for o in (4, 5, 6, 2, 1, 0):
            far_copy(o).start()

    @pl.when(me >= REACH)
    def _():
        send_table()

    for g in range(3):
        arrive(g, steps[g])
    lax.fori_loop(0, 5, near_phase, jnp.zeros((COLS, LEAF), f32))
    near_reply(HOME)

    for leaf in range(LEAVES):
        total = own_sum[leaf] + near_send[HOME, leaf]
        for u in range(NEAR_PER):
            total = total + near_own[plan[2, leaf * NEAR_PER + u]]
        own_sum[leaf] = total
    for j in range(1, sides):
        interp_copy(j).wait_recv()
    for m in range(4):
        ih[m], il[m] = split(gathered[m].reshape(128, LEAF))
    for o in others:
        far_copy(o).wait_recv()
    total = far_send[REACH]
    for o in others:
        total = total + far_recv[o]
    for m in range(4):
        far_sum[m * 8:(m + 1) * 8, :] = total[:, m * 128:(m + 1) * 128]
    fours = total[0:4, 512:640]
    parent = jnp.concatenate([fours, pltpu.roll(fours, SKEL, 1)], axis=0) + far_own[LEAVES]
    parent = stacked(parent[:, :SKEL])
    handed = folded(mul(parent, th[...]) + mul(parent, tl[...]))
    for m in range(4):
        down = handed[:, m * 128:(m + 1) * 128]
        even = far_sum[pl.ds(2 * m, 4, stride=8), :]
        odd = far_sum[pl.ds(2 * m + 1, 4, stride=8), :]
        even = jnp.concatenate([even, pltpu.roll(even, SKEL, 1)], axis=0) + far_own[2 * m] + down
        odd = jnp.concatenate([pltpu.roll(odd, SKEL, 1), odd], axis=0) + far_own[2 * m + 1] + down
        zero = jnp.zeros_like(even)
        both = jnp.concatenate([stacked(jnp.where(left, even, zero)), stacked(jnp.where(left, zero, odd))], axis=0)
        got = mul(both, ih[m]) + mul(both, il[m])
        for u in range(2):
            own_sum[2 * m + u] = own_sum[2 * m + u] + folded(got[16 * u:16 * u + 16])

    for o in others:
        reply_copy(0, o - REACH).wait_recv()
    for leaf in range(LEAVES):
        total = own_sum[leaf]
        for o in others:
            total = total + near_recv[o, leaf]
        out[:, leaf * LEAF:(leaf + 1) * LEAF] = COUPLE * total


    for copy in mix_copies + data_copies + skel_copies + part_copies:
        copy.wait_send()
    for j in range(1, sides):
        interp_copy(j).wait_send()
    for o in others:
        table_copy(0, o - REACH).wait_send()
        reply_copy(0, o - REACH).wait_send()
        far_copy(o).wait_send()


def shards(
    leaf_coords, charges, leaf_skeleton, parent_skeleton, interp, transfer,
    near_offset, near_partner, near_count, far_offset, far_partner,
):
    boxes, sides = lax.axis_size("box"), lax.axis_size("rhs")
    V, S, M = pltpu.VMEM, pltpu.SemaphoreType.DMA, pltpu.SMEM
    operands = (
        leaf_coords, charges, leaf_skeleton, parent_skeleton, interp, transfer,
        near_offset.reshape(1, -1), near_partner, near_count, far_offset.reshape(1, -1), far_partner,
    )
    return pl.pallas_call(
        functools.partial(kernel, boxes, sides),
        out_shape=jax.ShapeDtypeStruct(charges.shape, f32),
        in_specs=[pl.BlockSpec(memory_space=pltpu.HBM)] * len(operands),
        out_specs=pl.BlockSpec(memory_space=pltpu.VMEM),
        scratch_shapes=[
            V((SPAN, LEAVES, COLS, LEAF), f32),
            V((SPAN, LEAVES, 3, LEAF), f32),
            V((SPAN * LEAVES, COLS, LEAF), f32),
            V((SPAN * LEAVES, 3, LEAF), f32),
            V((4, COLS, 2 * LEAF), f32),
            V((4, COLS, 256), f32),
            V((32, 256), f32),
            V((SKEL, 512), bf16),
            V((SKEL, 512), bf16),
        ]
        + [V(a.shape, f32) for a in (charges, leaf_coords, leaf_skeleton, parent_skeleton, transfer)]
        + [M(a.shape, i32) for a in operands[6:]]
        + [
            V((8, 128), i32),
            M((8, 128), i32),
            V((SPAN, 3, TABLE), f32),
            V((SPAN, COLS, TABLE), f32),
            V((SPAN, LEAVES, COLS, LEAF), f32),
            V((SPAN, LEAVES, COLS, LEAF), f32),
            V((SPAN, 8, TABLE), f32),
            V((SPAN, 8, TABLE), f32),
            V((4, 2, SKEL, LEAF), f32),
            V((3, LEAVES, LEAF, 128), f32),
            V((3, ENTRIES * SKEL, 128), f32),
            V((LEAVES, 16, LEAF), bf16),
            V((LEAF, LEAF), bf16),
            V((LEAF, LEAF), bf16),
            V((LEAF, LEAF), bf16),
            V((LEAF, LEAF), bf16),
            V((NEAR_ROWS, COLS, LEAF), f32),
            V((NEAR_ROWS, COLS, LEAF), f32),
            V((LEAVES, COLS, LEAF), f32),
            V((128, 128), bf16),
            V((64, 16, 128), f32),
            V((64, 16, 128), f32),
            V((3, 128, FAR_PER * SKEL), bf16),
            V((3, 16, FAR_PER * SKEL), bf16),
            V((512, 128), f32),
            V((ENTRIES, 8, 128), f32),
            V((128, 1024), bf16),
            V((4, 128, LEAF), bf16),
            V((4, 128, LEAF), bf16),
            V((32, 128), f32),
            S((11,)), S(()), S((3,)), S((3,)), S((3,)), S((3,)), S((3,)), S((3,)), S((3, SPAN)), S((3, SPAN)), S((SPAN,)), S((SPAN,)),
            S((SPAN,)), S((SPAN,)), S((SPAN,)), S((SPAN,)),
        ],
        compiler_params=pltpu.CompilerParams(
            collective_id=0, has_side_effects=True, vmem_limit_bytes=60 * 2**20
        ),
    )(*operands)


def solution(mesh):
    return jax.shard_map(
        shards,
        mesh=mesh,
        in_specs=(
            P(None, "box"),
            P("rhs", "box"),
            P(None, "box"),
            P(None, "box"),
            P(("box", "rhs"), None, None),
            P("box", None, None),
            P(),
            P(),
            P(),
            P(),
            P(),
        ),
        out_specs=P("rhs", "box"),
        check_vma=False,
    )
```
